32 devices in a mesh: ctx: 16 (over z, y, x), tp: 2 (over core).
Axes of the slice: x: 2, y: 2, z: 4, core: 2. Of those that a mesh axis runs over, the one named last changes fastest.
Arguments:
- tokens: bfloat16 [4096, 896], P('ctx'), may hold values from -6 to 6
- attn_gain: bfloat16 [896], replicated, may hold values from 0.5 to 1.5
- w_query: bfloat16 [896, 896], P(None, 'tp'), may hold values from -0.1875 to 0.1875
- b_query: bfloat16 [896], P('tp'), may hold values from -3 to 3
- w_key: bfloat16 [896, 128], P(None, 'tp'), may hold values from -0.1875 to 0.1875
- b_key: bfloat16 [128], P('tp'), may hold values from -3 to 3
- w_value: bfloat16 [896, 128], P(None, 'tp'), may hold values from -0.1875 to 0.1875
- b_value: bfloat16 [128], P('tp'), may hold values from -3 to 3
- w_out: bfloat16 [896, 896], P('tp'), may hold values from -3 to 3
- mlp_gain: bfloat16 [896], replicated, may hold values from 0.5 to 1.5
- w_gate: bfloat16 [896, 4864], P(None, 'tp'), may hold values from -0.1875 to 0.1875
- w_up: bfloat16 [896, 4864], P(None, 'tp'), may hold values from -0.1875 to 0.1875
- w_down: bfloat16 [4864, 896], P('tp'), may hold values from -0.15625 to 0.15625
- cotangent: bfloat16 [4096, 896], P('ctx'), may hold values from -6 to 6
- block_table: int32 [16], replicated, may hold values from 0 to 15, each once
- doc_lengths: int32 [2, 6], replicated, may hold values from 1 to 1536, as said below
Outputs:
- mixed: bfloat16 [4096, 896], P('ctx')
- grad_tokens: float32 [4096, 896], P('ctx')
- grad_attn_gain: float32 [896], replicated
- grad_w_query: float32 [896, 896], P('ctx', 'tp')
- grad_b_query: float32 [896], P('tp')
- grad_w_key: float32 [896, 128], P('ctx', 'tp')
- grad_b_key: float32 [128], P('tp')
- grad_w_value: float32 [896, 128], P('ctx', 'tp')
- grad_b_value: float32 [128], P('tp')
- grad_w_out: float32 [896, 896], P('tp', 'ctx')
- grad_mlp_gain: float32 [896], replicated
- grad_w_gate: float32 [896, 4864], P('ctx', 'tp')
- grad_w_up: float32 [896, 4864], P('ctx', 'tp')
- grad_w_down: float32 [4864, 896], P('tp', 'ctx')
The draws below stay inside these ranges and needn't reach their ends.
Inputs may be any that keep to these rules, and one draw needn't show every extreme that they name: A permutation: index c of ctx holds blocks block_table[c] and 31 - block_table[c] of every sequence. `doc_lengths`: each row sums to 2048; the first document of every sequence holds at least half of its tokens and is its longest.
All inputs are finite; a program needn't handle non-finite values.
Results may differ from the reference program's by a relative error of at most 0.04.
Values may be sent and summed in bfloat16 or wider, within the bound.
A program may use at most 192 MiB of HBM per device.

```python
import jax
import jax.numpy as jnp
from jax import lax

D = 896
HEADS = 14
KVH = 2
HD = 64
FF = 4864
SEQS = 2
BLK = 64
DOCS = 6
SEQ_LEN = 2048
TOKENS = 4096
N_CTX = 16


def draw_doc_lengths(key, part):
    key = jax.random.fold_in(key, 7)
    first_key, rest_key, pick_key = jax.random.split(key, 3)
    longest = SEQ_LEN // 2 + SEQ_LEN // 4
    drawn_first = SEQ_LEN // 2 + jax.random.randint(first_key, (SEQS,), 0, SEQ_LEN // 4 + 1)
    chosen = jax.random.randint(pick_key, (), 0, SEQS)
    first_len = jnp.where(jnp.arange(SEQS) == chosen, longest, drawn_first)
    remain = SEQ_LEN - first_len
    portion = remain // (DOCS - 1)
    jitter = jax.random.randint(rest_key, (SEQS, DOCS - 2), -(portion // 2)[:, None], 1)
    middle = portion[:, None] + jitter
    last_len = remain - jnp.sum(middle, axis=1)
    return jnp.concatenate([first_len[:, None], middle, last_len[:, None]], axis=1).astype(jnp.int32)


def spiked(values, key, source, target, shards_of, factor):
    def block_of(axis_at):
        return (jnp.arange(values.shape[axis_at]) // (values.shape[axis_at] // shards_of)).reshape((-1,) + (1,) * (values.ndim - 1 - axis_at))

    near = jax.random.permutation(key, shards_of)[block_of(target)]
    far = (block_of(target) + shards_of // 2) % shards_of
    return jnp.where((block_of(source) == near) | (block_of(source) == far), factor * values, values)


def levels(own_key, dims, shards, low, largest):
    gain, own = 1.0, jax.random.fold_in(own_key, 6)
    for position, parts in shards:
        draws = jnp.exp(jax.random.uniform(jax.random.fold_in(own, position), (parts,), jnp.float32, low / len(shards), largest / len(shards)))
        gain = gain * jnp.repeat(draws, dims[position] // parts).reshape([-1 if axis == position else 1 for axis in range(len(dims))])
    return gain


def noise(stream_key, extent, deviation, bound, pieces=(), held_as=jnp.bfloat16):
    entries = deviation * jax.random.normal(stream_key, extent, jnp.float32)
    if pieces:
        entries = entries * levels(stream_key, extent, pieces, -0.22, 0.18)
    return jnp.clip(entries, -bound, bound).astype(held_as)


def gaussian_with(rng, extent, scale, bound, cuts, heavy, held_as=jnp.bfloat16):
    array = scale * jax.random.normal(rng, extent, jnp.float32)
    if cuts:
        array = array * levels(rng, extent, cuts, -0.22, 0.18)
    return jnp.clip(spiked(array, jax.random.fold_in(rng, 3), *heavy), -bound, bound).astype(held_as)


def setup_inputs(seed: int = 0) -> dict:
    key_list = jax.random.split(jax.random.key(seed), 17)
    tokens = gaussian_with(key_list[0], (TOKENS, D), 1.0, 6.0, ((0, 16),), (0, 1, 16, 2.0))
    attn_gain = jnp.clip(1.0 + 0.1 * jax.random.normal(key_list[1], (D,), jnp.float32), 0.5, 1.5).astype(jnp.bfloat16)
    w_query = noise(key_list[2], (D, HEADS * HD), D ** -0.5, 0.1875, ((1, 2),))
    b_query = noise(key_list[3], (HEADS * HD,), 0.5, 3.0, ((0, 2),))
    w_key = noise(key_list[4], (D, KVH * HD), D ** -0.5, 0.1875, ((1, 2),))
    b_key = noise(key_list[5], (KVH * HD,), 0.5, 3.0, ((0, 2),))
    w_value = noise(key_list[6], (D, KVH * HD), D ** -0.5, 0.1875, ((1, 2),))
    b_value = noise(key_list[7], (KVH * HD,), 0.5, 3.0, ((0, 2),))
    w_out = noise(key_list[8], (HEADS * HD, D), 4 ** -0.5, 3.0, ((0, 2),))
    mlp_gain = jnp.clip(1.0 + 0.1 * jax.random.normal(key_list[9], (D,), jnp.float32), 0.5, 1.5).astype(jnp.bfloat16)
    w_gate = noise(key_list[10], (D, FF), D ** -0.5, 0.1875, ((1, 2),))
    w_up = noise(key_list[11], (D, FF), D ** -0.5, 0.1875, ((1, 2),))
    w_down = noise(key_list[12], (FF, D), (FF // 4) ** -0.5, 0.15625, ((0, 2),))
    cotangent = noise(key_list[13], (TOKENS, D), 1.0, 6.0, ((0, 16),))
    block_table = jax.random.permutation(key_list[14], N_CTX).astype(jnp.int32)
    doc_lengths = draw_doc_lengths(jax.random.fold_in(key_list[16], 71), 0)
    return dict(tokens=tokens, attn_gain=attn_gain, w_query=w_query, b_query=b_query, w_key=w_key, b_key=b_key, w_value=w_value, b_value=b_value, w_out=w_out, mlp_gain=mlp_gain, w_gate=w_gate, w_up=w_up, w_down=w_down, cotangent=cotangent, block_table=block_table, doc_lengths=doc_lengths)


@jax.custom_vjp
def low(v):
    return lax.optimization_barrier(v.astype(jnp.bfloat16)).astype(jnp.float32)

@jax.custom_vjp
def low_back(v):
    return v

def low_keep(v):
    return (low(v), None)

def low_pass(kept, grad):
    return (grad,)

def back_keep(v):
    return (v, None)

def back_low(kept, grad):
    return (low(grad),)
low.defvjp(low_keep, low_pass)
low_back.defvjp(back_keep, back_low)
EPSILON = 1e-06
THETA = 1000000.0
NEGATIVE = -1e+30
HIGHEST = lax.Precision.HIGHEST

def matmul(left, right):
    return jnp.dot(left, right, precision=HIGHEST)

def rope_tables(positions, head_width):
    half_width = head_width // 2
    frequency = THETA ** (-jnp.arange(half_width, dtype=jnp.float32) * 2.0 / head_width)
    angles = positions.astype(jnp.float32)[:, None] * frequency[None, :]
    return (jnp.cos(angles), jnp.sin(angles))

def rotate(values, cos_table, sin_table):
    half_width = values.shape[-1] // 2
    cos_part = cos_table[:, None, :]
    sin_part = sin_table[:, None, :]
    first_half = values[..., :half_width]
    second_half = values[..., half_width:]
    return jnp.concatenate([first_half * cos_part - second_half * sin_part, second_half * cos_part + first_half * sin_part], axis=-1)

def attend_block(query_block, query_pos, query_seg, key_seq, value_seq, key_pos, key_seg):
    row_count = query_block.shape[0]
    grouped = query_block.reshape(row_count, KVH, HEADS // KVH, HD)
    scores = low_back(jnp.einsum('rkgd,lkd->kgrl', grouped, key_seq, precision=HIGHEST) * HD ** (-0.5))
    allowed = (key_pos[None, :] <= query_pos[:, None]) & (key_seg[None, :] == query_seg[:, None])
    masked = jnp.where(allowed[None, None], scores, NEGATIVE)
    highest = lax.optimization_barrier(jnp.max(masked, axis=3, keepdims=True))
    raised = jnp.exp(masked - highest)
    shares = low(raised / lax.optimization_barrier(jnp.sum(raised, axis=3, keepdims=True)))
    mixed_heads = jnp.einsum('kgrl,lkd->rkgd', shares, value_seq, precision=HIGHEST)
    return mixed_heads.reshape(row_count, HEADS * HD)

def attend_sequence(query_seq, key_seq, value_seq, seq_segs, positions):
    block_rows = min(512, SEQ_LEN)
    blocks = SEQ_LEN // block_rows
    stepper = jax.checkpoint(attend_block)

    def one_block(members):
        return stepper(members[0], members[1], members[2], key_seq, value_seq, positions, seq_segs)
    result = lax.map(one_block, (query_seq.reshape(blocks, block_rows, HEADS, HD), positions.reshape(blocks, block_rows), seq_segs.reshape(blocks, block_rows)))
    return result.reshape(SEQ_LEN, HEADS * HD)

def reference(tokens, attn_gain, w_query, b_query, w_key, b_key, w_value, b_value, w_out, mlp_gain, w_gate, w_up, w_down, cotangent, block_table, doc_lengths):
    firsts = block_table.astype(jnp.int32)
    pair_blocks = jnp.stack([firsts, 2 * N_CTX - 1 - firsts], axis=1)
    positions = (pair_blocks[:, :, None] * BLK + jnp.arange(BLK, dtype=jnp.int32)[None, None, :]).reshape(SEQ_LEN)
    bounds = jnp.cumsum(doc_lengths.astype(jnp.int32), axis=1)
    segments = lax.optimization_barrier(jnp.sum((positions[None, :, None] >= bounds[:, None, :]).astype(jnp.int32), axis=2))
    cos_table, sin_table = rope_tables(positions, HD)

    def to_sequences(rows, heads_here):
        return rows.reshape(N_CTX, SEQS, 2 * BLK, heads_here, HD).transpose(1, 0, 2, 3, 4).reshape(SEQS, SEQ_LEN, heads_here, HD)

    def forward(tokens_in, gain_one, query_w, query_b, key_w, key_b, value_w, value_b, out_w, gain_two, gate_w, up_w, down_w):
        inv_one = lax.rsqrt(lax.optimization_barrier(jnp.mean(tokens_in * tokens_in, axis=1, keepdims=True)) + EPSILON)
        normed = low(tokens_in * inv_one * gain_one)
        query_rows = low_back(matmul(normed, query_w) + query_b)
        key_rows = low_back(matmul(normed, key_w) + key_b)
        values = low(low_back(matmul(normed, value_w) + value_b))
        query_seq = low(rotate(to_sequences(query_rows, HEADS), cos_table, sin_table))
        key_seq = low(rotate(to_sequences(key_rows, KVH), cos_table, sin_table))
        value_seq = to_sequences(values, KVH)

        def per_sequence(members):
            return attend_sequence(members[0], members[1], members[2], members[3], positions)
        attended = lax.map(per_sequence, (query_seq, key_seq, value_seq, segments))
        attn_rows = attended.reshape(SEQS, N_CTX, 2 * BLK, HEADS * HD).transpose(1, 0, 2, 3).reshape(TOKENS, HEADS * HD)
        attn_low = low(low_back(attn_rows))
        branch = low_back(matmul(attn_low, out_w))
        stream = tokens_in + branch
        inv_two = lax.rsqrt(lax.optimization_barrier(jnp.mean(stream * stream, axis=1, keepdims=True)) + EPSILON)
        normed_two = low(stream * inv_two * gain_two)
        gate_pre = low_back(matmul(normed_two, gate_w))
        upward = low_back(matmul(normed_two, up_w))
        hidden = low(jax.nn.silu(gate_pre) * upward)
        return stream + matmul(hidden, down_w)
    floats = [operand.astype(jnp.float32) for operand in (tokens, attn_gain, w_query, b_query, w_key, b_key, w_value, b_value, w_out, mlp_gain, w_gate, w_up, w_down)]
    mixed, pullback = jax.vjp(forward, *floats)
    gradients = pullback(cotangent.astype(jnp.float32))
    return (mixed.astype(jnp.bfloat16), gradients[0], gradients[1], gradients[2], gradients[3], gradients[4], gradients[5], gradients[6], gradients[7], gradients[8], gradients[9], gradients[10], gradients[11], gradients[12])
```

```python
import jax
import jax.numpy as jnp
from jax import lax
from jax.sharding import PartitionSpec as P

EPSILON = 1e-06
THETA = 1000000.0
NEGATIVE = -1e30
KEY_BLOCK = 1024


def rope_tables(positions, head_width):
    half_width = head_width // 2
    frequency = THETA ** (-jnp.arange(half_width, dtype=jnp.float32) * 2.0 / head_width)
    angles = positions.astype(jnp.float32)[:, None] * frequency[None, :]
    return (jnp.cos(angles), jnp.sin(angles))


def rotate(values, cos_table, sin_table):
    half_width = values.shape[-1] // 2
    cos_part = cos_table[:, None, :]
    sin_part = sin_table[:, None, :]
    first_half = values[..., :half_width]
    second_half = values[..., half_width:]
    return jnp.concatenate(
        [
            first_half * cos_part - second_half * sin_part,
            second_half * cos_part + first_half * sin_part,
        ],
        axis=-1,
    )


def norm_back(grad_normed, inputs, inverse, gain_f):
    scaled = grad_normed * gain_f
    grad_in = inverse * scaled - inputs * (inverse * inverse * inverse) * jnp.mean(
        scaled * inputs, axis=1, keepdims=True
    )
    grad_gain = jnp.sum(grad_normed * inputs * inverse, axis=0)
    return (grad_in, grad_gain)


def swap(values, axis_name, bit):
    size = lax.axis_size(axis_name)
    return lax.ppermute(values, axis_name, [(i, i ^ bit) for i in range(size)])


def sum_pair(part):
    low = part.astype(jnp.bfloat16)
    return low.astype(jnp.float32) + swap(low, "tp", 1).astype(jnp.float32)


def bit_list(count):
    return [1 << b for b in range(count.bit_length() - 1)]


def scatter_rows(matrix, order):
    index = lax.axis_index("ctx")
    count = lax.axis_size("ctx")
    rows, columns = matrix.shape
    block = rows // count
    cur = matrix
    left = sorted(order, reverse=True)
    for bit in order:
        at = left.index(bit)
        before = 1 << at
        after = 1 << (len(left) - at - 1)
        shaped = cur.reshape(before, 2, after * block, columns)
        mine = (index // bit) % 2
        keep = lax.dynamic_index_in_dim(shaped, mine, 1, keepdims=False)
        send = lax.dynamic_index_in_dim(shaped, 1 - mine, 1, keepdims=False)
        got = swap(send, "ctx", bit)
        total = keep.astype(jnp.float32) + got.astype(jnp.float32)
        left.remove(bit)
        if left:
            cur = total.astype(jnp.bfloat16).reshape(before * after * block, columns)
        else:
            cur = total.reshape(block, columns)
    return cur


def shards(
    tokens,
    attn_gain,
    w_query,
    b_query,
    w_key,
    b_key,
    w_value,
    b_value,
    w_out,
    mlp_gain,
    w_gate,
    w_up,
    w_down,
    cotangent,
    block_table,
    doc_lengths,
):
    tok_rows, model_width = tokens.shape
    head_dim = w_key.shape[1]
    group = w_query.shape[1] // head_dim
    seq_count = doc_lengths.shape[0]
    half_rows = tok_rows // seq_count
    block_len = half_rows // 2
    ctx_size = lax.axis_size("ctx")
    seq_len = ctx_size * half_rows
    scale = head_dim ** (-0.5)
    query_rows_all = group * half_rows
    own_index = lax.axis_index("ctx")
    pair_blocks = jnp.stack([block_table, 2 * ctx_size - 1 - block_table], axis=1)
    all_pos = (
        pair_blocks[:, :, None] * block_len + jnp.arange(block_len, dtype=jnp.int32)[None, None, :]
    ).reshape(seq_len)
    own_pos = lax.dynamic_slice_in_dim(all_pos, own_index * half_rows, half_rows)
    bits = bit_list(ctx_size)
    masks = [0]
    for bit in reversed(bits):
        masks = masks + [m ^ bit for m in masks]
    slots = jnp.array(masks, jnp.int32) ^ own_index
    all_pos = all_pos.reshape(ctx_size, half_rows)[slots].reshape(seq_len)
    bounds = jnp.cumsum(doc_lengths, axis=1)
    all_seg = jnp.sum((all_pos[None, :, None] >= bounds[:, None, :]).astype(jnp.int32), axis=2)
    own_seg = all_seg[:, :half_rows]
    cos_table, sin_table = rope_tables(own_pos, head_dim)
    query_pos = jnp.tile(own_pos, group)
    query_seg = jnp.tile(own_seg, (1, group))
    x_float = tokens.astype(jnp.float32)
    gain_one = attn_gain.astype(jnp.float32)
    gain_two = mlp_gain.astype(jnp.float32)
    inv_one = lax.rsqrt(jnp.mean(x_float * x_float, axis=1, keepdims=True) + EPSILON)
    normed = (x_float * inv_one * gain_one).astype(jnp.bfloat16)
    query_pre = jnp.dot(normed, w_query, preferred_element_type=jnp.float32) + b_query.astype(
        jnp.float32
    )
    key_pre = jnp.dot(normed, w_key, preferred_element_type=jnp.float32) + b_key.astype(jnp.float32)
    value_rows = (
        jnp.dot(normed, w_value, preferred_element_type=jnp.float32) + b_value.astype(jnp.float32)
    ).astype(jnp.bfloat16)
    query_rot = rotate(
        query_pre.reshape(seq_count, half_rows, group, head_dim), cos_table, sin_table
    ).astype(jnp.bfloat16)
    query_heads = query_rot.transpose(0, 2, 1, 3).reshape(seq_count, query_rows_all, head_dim)
    key_local = (
        rotate(key_pre.reshape(seq_count, half_rows, 1, head_dim), cos_table, sin_table)
        .reshape(seq_count, half_rows, head_dim)
        .astype(jnp.bfloat16)
    )
    value_local = value_rows.reshape(seq_count, half_rows, head_dim)

    def masked_scores(key_block, start):
        count = key_block.shape[1]
        key_pos = lax.dynamic_slice_in_dim(all_pos, start, count)
        key_seg = lax.dynamic_slice_in_dim(all_seg, start, count, axis=1)
        scores = (
            jnp.einsum("sqd,skd->sqk", query_heads, key_block, preferred_element_type=jnp.float32)
            * scale
        )
        allowed = (key_pos[None, None, :] <= query_pos[None, :, None]) & (
            key_seg[:, None, :] == query_seg[:, :, None]
        )
        return (scores, allowed)

    def absorb(carry, key_block, value_block, start):
        run_max, run_sum, run_acc = carry
        scores, allowed = masked_scores(key_block, start)
        new_max = jnp.maximum(run_max, jnp.max(jnp.where(allowed, scores, NEGATIVE), axis=2))
        weights = jnp.where(allowed, jnp.exp(scores - new_max[:, :, None]), 0.0)
        factor = jnp.exp(run_max - new_max)
        run_sum = run_sum * factor + jnp.sum(weights, axis=2)
        run_acc = run_acc * factor[:, :, None] + jnp.einsum(
            "sqk,skd->sqd",
            weights.astype(jnp.bfloat16),
            value_block,
            preferred_element_type=jnp.float32,
        )
        return (new_max, run_sum, run_acc)

    initial = (
        jnp.full((seq_count, query_rows_all), NEGATIVE, jnp.float32),
        jnp.zeros((seq_count, query_rows_all), jnp.float32),
        jnp.zeros((seq_count, query_rows_all, head_dim), jnp.float32),
    )
    gathered = jnp.concatenate([key_local, value_local], axis=2)
    for bit in reversed(bits):
        gathered = jnp.concatenate([gathered, swap(gathered, "ctx", bit)], axis=1)
    key_piece = gathered[:, :, :head_dim]
    value_piece = gathered[:, :, head_dim:]
    count = key_piece.shape[1]

    def inner(index_block, state):
        offset = index_block * KEY_BLOCK
        key_block = lax.dynamic_slice_in_dim(key_piece, offset, KEY_BLOCK, axis=1)
        value_block = lax.dynamic_slice_in_dim(value_piece, offset, KEY_BLOCK, axis=1)
        return absorb(state, key_block, value_block, offset)

    final_state = lax.fori_loop(0, count // KEY_BLOCK, inner, initial)
    run_max, run_sum, run_acc = final_state
    attended = run_acc / run_sum[:, :, None]
    log_total = run_max + jnp.log(run_sum)
    attn_rows = (
        attended.reshape(seq_count, group, half_rows, head_dim)
        .transpose(0, 2, 1, 3)
        .reshape(tok_rows, group * head_dim)
    )
    attn_low = attn_rows.astype(jnp.bfloat16)
    branch = sum_pair(jnp.dot(attn_low, w_out, preferred_element_type=jnp.float32))
    stream = x_float + branch
    inv_two = lax.rsqrt(jnp.mean(stream * stream, axis=1, keepdims=True) + EPSILON)
    normed_two = (stream * inv_two * gain_two).astype(jnp.bfloat16)
    gate_pre = jnp.dot(normed_two, w_gate, preferred_element_type=jnp.float32)
    upward = jnp.dot(normed_two, w_up, preferred_element_type=jnp.float32)
    sigmoid_gate = jax.nn.sigmoid(gate_pre)
    swish = gate_pre * sigmoid_gate
    hidden = (swish * upward).astype(jnp.bfloat16)
    down_part = sum_pair(jnp.dot(hidden, w_down, preferred_element_type=jnp.float32))
    mixed = (stream + down_part).astype(jnp.bfloat16)
    grad_f = cotangent.astype(jnp.float32)
    grad_w_down = jnp.dot(cotangent.T, hidden, preferred_element_type=jnp.float32)
    grad_hidden = jnp.dot(cotangent, w_down.T, preferred_element_type=jnp.float32)
    grad_gate_low = (
        grad_hidden * upward * sigmoid_gate * (1.0 + gate_pre * (1.0 - sigmoid_gate))
    ).astype(jnp.bfloat16)
    grad_up_low = (grad_hidden * swish).astype(jnp.bfloat16)
    grad_w_gate = jnp.dot(normed_two.T, grad_gate_low, preferred_element_type=jnp.float32)
    grad_w_up = jnp.dot(normed_two.T, grad_up_low, preferred_element_type=jnp.float32)
    grad_normed_part = jnp.dot(
        grad_gate_low, w_gate.T, preferred_element_type=jnp.float32
    ) + jnp.dot(grad_up_low, w_up.T, preferred_element_type=jnp.float32)
    grad_normed_two = sum_pair(grad_normed_part)
    grad_stream_part, grad_mlp_gain = norm_back(grad_normed_two, stream, inv_two, gain_two)
    grad_stream = grad_f + grad_stream_part
    grad_branch = grad_stream.astype(jnp.bfloat16)
    grad_w_out = jnp.dot(grad_branch.T, attn_low, preferred_element_type=jnp.float32)
    grad_attn_low = jnp.dot(grad_branch, w_out.T, preferred_element_type=jnp.float32).astype(
        jnp.bfloat16
    )
    grad_heads = (
        grad_attn_low.reshape(seq_count, half_rows, group, head_dim)
        .transpose(0, 2, 1, 3)
        .reshape(seq_count, query_rows_all, head_dim)
    )
    delta = jnp.sum(grad_heads.astype(jnp.float32) * attended, axis=2)
    back_keys, back_values = (key_piece, value_piece)
    key_block_len = min(KEY_BLOCK, seq_len)
    block_count = seq_len // key_block_len

    def back_block(grad_query_acc, index_block):
        offset = index_block * key_block_len
        key_block = lax.dynamic_slice_in_dim(back_keys, offset, key_block_len, axis=1)
        value_block = lax.dynamic_slice_in_dim(back_values, offset, key_block_len, axis=1)
        scores, allowed = masked_scores(key_block, offset)
        shares = jnp.where(allowed, jnp.exp(scores - log_total[:, :, None]), 0.0)
        grad_value_block = jnp.einsum(
            "sqk,sqd->skd",
            shares.astype(jnp.bfloat16),
            grad_heads,
            preferred_element_type=jnp.float32,
        )
        grad_shares = jnp.einsum(
            "sqd,skd->sqk", grad_heads, value_block, preferred_element_type=jnp.float32
        )
        grad_scores = (shares * (grad_shares - delta[:, :, None])).astype(jnp.bfloat16)
        grad_query_acc = (
            grad_query_acc
            + jnp.einsum("sqk,skd->sqd", grad_scores, key_block, preferred_element_type=jnp.float32)
            * scale
        )
        grad_key_block = (
            jnp.einsum("sqk,sqd->skd", grad_scores, query_heads, preferred_element_type=jnp.float32)
            * scale
        )
        return (grad_query_acc, (grad_key_block, grad_value_block))

    grad_query_heads, (grad_key_blocks, grad_value_blocks) = lax.scan(
        back_block,
        jnp.zeros((seq_count, query_rows_all, head_dim), jnp.float32),
        jnp.arange(block_count),
    )
    grad_keys_all = jnp.moveaxis(grad_key_blocks, 0, 1).reshape(seq_count, seq_len, head_dim)
    grad_values_all = jnp.moveaxis(grad_value_blocks, 0, 1).reshape(seq_count, seq_len, head_dim)
    cur = jnp.concatenate([grad_keys_all, grad_values_all], axis=2).astype(jnp.bfloat16)
    for bit in bits:
        half = cur.shape[1] // 2
        total = cur[:, :half].astype(jnp.float32) + swap(cur[:, half:], "ctx", bit).astype(
            jnp.float32
        )
        cur = total if bit == bits[-1] else total.astype(jnp.bfloat16)
    grad_keys_own = cur[:, :, :head_dim]
    grad_values_own = cur[:, :, head_dim:]
    grad_query_rows = grad_query_heads.reshape(seq_count, group, half_rows, head_dim).transpose(
        0, 2, 1, 3
    )
    grad_query_low = (
        rotate(grad_query_rows, cos_table, -sin_table)
        .reshape(tok_rows, group * head_dim)
        .astype(jnp.bfloat16)
    )
    grad_key_low = (
        rotate(grad_keys_own.reshape(seq_count, half_rows, 1, head_dim), cos_table, -sin_table)
        .reshape(tok_rows, head_dim)
        .astype(jnp.bfloat16)
    )
    grad_value_low = grad_values_own.reshape(tok_rows, head_dim).astype(jnp.bfloat16)
    grad_w_query = jnp.dot(normed.T, grad_query_low, preferred_element_type=jnp.float32)
    grad_w_key = jnp.dot(normed.T, grad_key_low, preferred_element_type=jnp.float32)
    grad_w_value = jnp.dot(normed.T, grad_value_low, preferred_element_type=jnp.float32)
    grad_b_query = jnp.sum(grad_query_low.astype(jnp.float32), axis=0)
    grad_b_key = jnp.sum(grad_key_low.astype(jnp.float32), axis=0)
    grad_b_value = jnp.sum(grad_value_low.astype(jnp.float32), axis=0)
    grad_first_part = (
        jnp.dot(grad_query_low, w_query.T, preferred_element_type=jnp.float32)
        + jnp.dot(grad_key_low, w_key.T, preferred_element_type=jnp.float32)
        + jnp.dot(grad_value_low, w_value.T, preferred_element_type=jnp.float32)
    )
    grad_normed = sum_pair(grad_first_part)
    grad_in_part, grad_attn_gain = norm_back(grad_normed, x_float, inv_one, gain_one)
    grad_tokens = grad_stream + grad_in_part
    other = [bits[1], bits[0]] + bits[2:]

    def scatter(matrix, order):
        return scatter_rows(matrix.astype(jnp.bfloat16), order)

    middle = grad_w_down.shape[1] // 2 // 128 * 128
    sum_down = jnp.concatenate(
        [scatter(grad_w_down[:, :middle], bits), scatter(grad_w_down[:, middle:], other)], axis=1
    ).T
    sum_gate = scatter(grad_w_gate, bits)
    sum_up = scatter(grad_w_up, other)
    sum_out = scatter(grad_w_out, bits).T
    first_cols = grad_w_query.shape[1]
    projections = scatter(jnp.concatenate([grad_w_query, grad_w_key, grad_w_value], axis=1), other)
    sum_query = projections[:, :first_cols]
    sum_key = projections[:, first_cols : first_cols + head_dim]
    sum_value = projections[:, first_cols + head_dim :]
    pieces = (grad_attn_gain, grad_mlp_gain, grad_b_query, grad_b_key, grad_b_value)
    flat = jnp.concatenate(pieces)
    padded = -(-flat.shape[0] // 1024) * 1024
    flat = jnp.pad(flat, (0, padded - flat.shape[0])).reshape(8, padded // 8)
    for bit in bits:
        flat = flat + swap(flat, "ctx", bit)
    flat = flat.reshape(padded)
    small = []
    begin = 0
    for piece in pieces:
        small.append(flat[begin : begin + piece.shape[0]])
        begin += piece.shape[0]
    return (
        mixed,
        grad_tokens,
        small[0],
        sum_query,
        small[2],
        sum_key,
        small[3],
        sum_value,
        small[4],
        sum_out,
        small[1],
        sum_gate,
        sum_up,
        sum_down,
    )


def solution(mesh):
    return jax.shard_map(
        shards,
        mesh=mesh,
        in_specs=(
            P("ctx", None),
            P(),
            P(None, "tp"),
            P("tp"),
            P(None, "tp"),
            P("tp"),
            P(None, "tp"),
            P("tp"),
            P("tp", None),
            P(),
            P(None, "tp"),
            P(None, "tp"),
            P("tp", None),
            P("ctx", None),
            P(),
            P(),
        ),
        out_specs=(
            P("ctx", None),
            P("ctx", None),
            P(),
            P("ctx", "tp"),
            P("tp"),
            P("ctx", "tp"),
            P("tp"),
            P("ctx", "tp"),
            P("tp"),
            P("tp", "ctx"),
            P(),
            P("ctx", "tp"),
            P("ctx", "tp"),
            P("tp", "ctx"),
        ),
        check_vma=False,
    )
```

```python
import functools

import jax
import jax.numpy as jnp
from jax import lax
from jax.experimental import pallas as pl
from jax.experimental.pallas import tpu as pltpu
from jax.sharding import PartitionSpec as P

EPSILON = 1e-06
THETA = 1000000.0
NEGATIVE = -1e30
KEY_BLOCK = 256
VMEM_BYTES = 40 * 1024 * 1024
CONTRACT_LAST = (((1,), (1,)), ((), ()))
CONTRACT_FIRST = (((0,), (0,)), ((), ()))


def rope_tables(positions, head_width):
    half_width = head_width // 2
    frequency = THETA ** (-jnp.arange(half_width, dtype=jnp.float32) * 2.0 / head_width)
    angles = positions.astype(jnp.float32)[:, None] * frequency[None, :]
    return (jnp.cos(angles), jnp.sin(angles))


def rotate(values, cos_table, sin_table):
    half_width = values.shape[-1] // 2
    cos_part = cos_table[:, None, :]
    sin_part = sin_table[:, None, :]
    first_half = values[..., :half_width]
    second_half = values[..., half_width:]
    return jnp.concatenate(
        [
            first_half * cos_part - second_half * sin_part,
            second_half * cos_part + first_half * sin_part,
        ],
        axis=-1,
    )


def norm_back(grad_normed, inputs, inverse, gain_f):
    scaled = grad_normed * gain_f
    grad_in = inverse * scaled - inputs * (inverse * inverse * inverse) * jnp.mean(
        scaled * inputs, axis=1, keepdims=True
    )
    grad_gain = jnp.sum(grad_normed * inputs * inverse, axis=0)
    return (grad_in, grad_gain)


def swap(values, axis_name, bit):
    size = lax.axis_size(axis_name)
    return lax.ppermute(values, axis_name, [(i, i ^ bit) for i in range(size)])


def sum_pair(part):
    low = part.astype(jnp.bfloat16)
    return low.astype(jnp.float32) + swap(low, "tp", 1).astype(jnp.float32)


def bit_list(count):
    return [1 << b for b in range(count.bit_length() - 1)]


def scatter_rows(matrix, order):
    index = lax.axis_index("ctx")
    count = lax.axis_size("ctx")
    rows, columns = matrix.shape
    block = rows // count
    cur = matrix
    left = sorted(order, reverse=True)
    for bit in order:
        at = left.index(bit)
        before = 1 << at
        after = 1 << (len(left) - at - 1)
        shaped = cur.reshape(before, 2, after * block, columns)
        mine = (index // bit) % 2
        keep = lax.dynamic_index_in_dim(shaped, mine, 1, keepdims=False)
        send = lax.dynamic_index_in_dim(shaped, 1 - mine, 1, keepdims=False)
        got = swap(send, "ctx", bit)
        total = keep.astype(jnp.float32) + got.astype(jnp.float32)
        left.remove(bit)
        if left:
            cur = total.astype(jnp.bfloat16).reshape(before * after * block, columns)
        else:
            cur = total.reshape(block, columns)
    return cur


def stack_heads(rows, head_dim):
    heads = rows.shape[1] // head_dim
    return jnp.concatenate(
        [rows[:, h * head_dim : (h + 1) * head_dim] for h in range(heads)], axis=0
    )


def unstack_heads(stacked, count):
    heads = stacked.shape[0] // count
    return jnp.concatenate([stacked[h * count : (h + 1) * count] for h in range(heads)], axis=1)


def sort_blocks(slot_ref, kv_ref, sorted_ref):
    blocks, block_len = kv_ref.shape[1], kv_ref.shape[2]

    def move(b, carry):
        sorted_ref[pl.ds(pl.multiple_of(b * block_len, block_len), block_len), :] = kv_ref[
            0, slot_ref[b]
        ]
        return carry

    lax.fori_loop(0, blocks, move, 0)


def forward_kernel(
    key_len, slot_ref, low_ref, high_ref, q_ref, kv_ref, pos_ref, first_ref,
    attn_ref, low_attn_ref, log_ref, sorted_ref,
):
    step = pl.program_id(0) * pl.num_programs(1) + pl.program_id(1)
    head_dim = kv_ref.shape[3] // 2
    count = q_ref.shape[0]

    @pl.when(pl.program_id(1) == 0)
    def _():
        sort_blocks(slot_ref, kv_ref, sorted_ref)

    queries = stack_heads(q_ref[...].astype(jnp.float32), head_dim).astype(jnp.bfloat16)
    rows = queries.shape[0]
    q_pos, q_first = pos_ref[0], first_ref[0]

    def body(j, carry):
        top, total, acc = carry
        start = pl.multiple_of(j * key_len, key_len)
        both = sorted_ref[pl.ds(start, key_len), :]
        keys, values = both[:, :head_dim], both[:, head_dim:]
        scores = lax.dot_general(keys, queries, CONTRACT_LAST, preferred_element_type=jnp.float32)
        k_pos = start + lax.broadcasted_iota(jnp.int32, scores.shape, 0)
        seen = (k_pos <= q_pos) & (k_pos >= q_first)
        scores = jnp.where(seen, scores, NEGATIVE)
        new_top = jnp.maximum(top, jnp.max(scores, axis=0, keepdims=True))
        weights = jnp.where(seen, jnp.exp(scores - new_top), 0.0)
        factor = jnp.exp(top - new_top)
        total = total * factor + jnp.sum(weights, axis=0, keepdims=True)
        acc = acc * factor + lax.dot_general(
            values, weights.astype(jnp.bfloat16), CONTRACT_FIRST,
            preferred_element_type=jnp.float32,
        )
        return new_top, total, acc

    init = (
        jnp.full((1, rows), NEGATIVE, jnp.float32),
        jnp.zeros((1, rows), jnp.float32),
        jnp.zeros((head_dim, rows), jnp.float32),
    )
    top, total, acc = lax.fori_loop(low_ref[step], high_ref[step], body, init)
    out = unstack_heads((acc / total).T, count)
    attn_ref[...] = out
    low_attn_ref[...] = out.astype(jnp.bfloat16)
    log_ref[0] = top + jnp.log(total)


def backward_kernel(
    key_len, scale, slot_ref, low_ref, high_ref, block_ref, q_ref, kv_ref, pos_ref, first_ref,
    attn_ref, log_ref, grad_ref, grad_q_ref, grad_kv_ref, sorted_ref, acc_ref,
):
    step = pl.program_id(0) * pl.num_programs(1) + pl.program_id(1)
    head_dim = kv_ref.shape[3] // 2
    blocks, block_len = kv_ref.shape[1], kv_ref.shape[2]
    count = q_ref.shape[0]

    @pl.when(pl.program_id(1) == 0)
    def _():
        sort_blocks(slot_ref, kv_ref, sorted_ref)
        acc_ref[...] = jnp.zeros_like(acc_ref)

    queries = stack_heads(q_ref[...].astype(jnp.float32), head_dim).astype(jnp.bfloat16)
    grad_f = grad_ref[...].astype(jnp.float32)
    grads = stack_heads(grad_f, head_dim).astype(jnp.bfloat16)
    delta = jnp.sum(stack_heads(grad_f * attn_ref[...], head_dim).T, axis=0, keepdims=True)
    rows = queries.shape[0]
    q_pos, q_first, log_total = pos_ref[0], first_ref[0], log_ref[0]

    def body(j, grad_q):
        start = pl.multiple_of(j * key_len, key_len)
        both = sorted_ref[pl.ds(start, key_len), :]
        keys, values = both[:, :head_dim], both[:, head_dim:]
        scores = lax.dot_general(keys, queries, CONTRACT_LAST, preferred_element_type=jnp.float32)
        k_pos = start + lax.broadcasted_iota(jnp.int32, scores.shape, 0)
        seen = (k_pos <= q_pos) & (k_pos >= q_first)
        shares = jnp.where(seen, jnp.exp(jnp.where(seen, scores - log_total, 0.0)), 0.0)
        grad_shares = lax.dot_general(
            values, grads, CONTRACT_LAST, preferred_element_type=jnp.float32
        )
        grad_scores = (shares * (grad_shares - delta)).astype(jnp.bfloat16)
        grad_values = jnp.dot(
            shares.astype(jnp.bfloat16), grads, preferred_element_type=jnp.float32
        )
        grad_keys = jnp.dot(grad_scores, queries, preferred_element_type=jnp.float32)
        acc_ref[pl.ds(start, key_len), :] += jnp.concatenate([grad_keys, grad_values], axis=1)
        return grad_q + lax.dot_general(
            keys, grad_scores, CONTRACT_FIRST, preferred_element_type=jnp.float32
        )

    grad_q = lax.fori_loop(
        low_ref[step], high_ref[step], body, jnp.zeros((head_dim, rows), jnp.float32)
    )
    grad_q_ref[...] = unstack_heads(grad_q.T, count) * scale

    @pl.when(pl.program_id(1) == pl.num_programs(1) - 1)
    def _():
        def move(k, carry):
            at = pl.multiple_of(block_ref[k] * block_len, block_len)
            grad_kv_ref[0, k] = acc_ref[pl.ds(at, block_len), :].astype(jnp.bfloat16)
            return carry

        lax.fori_loop(0, blocks, move, 0)


def attention(seq_count, key_len, head_dim, plan, queries, key_values, pos, first):
    rows, width = queries.shape
    blocks, block_len = key_values.shape[1:3]
    stacked = pos.shape[2]
    row_spec = pl.BlockSpec((block_len, width), lambda s, j, *_: (s * 2 + j, 0))
    kv_spec = pl.BlockSpec((1, blocks, block_len, 2 * head_dim), lambda s, j, *_: (s, 0, 0, 0))
    lane_spec = pl.BlockSpec((1, 1, stacked), lambda s, j, *_: (s * 2 + j, 0, 0))
    flops = 2 * 2 * rows * width * blocks * block_len // 2
    sorted_shape = pltpu.VMEM((blocks * block_len, 2 * head_dim), jnp.bfloat16)
    params = pltpu.CompilerParams(vmem_limit_bytes=VMEM_BYTES)

    def forward():
        return pl.pallas_call(
            functools.partial(forward_kernel, key_len),
            grid_spec=pltpu.PrefetchScalarGridSpec(
                num_scalar_prefetch=3,
                grid=(seq_count, 2),
                in_specs=[row_spec, kv_spec, lane_spec, lane_spec],
                out_specs=[row_spec, row_spec, lane_spec],
                scratch_shapes=[sorted_shape],
            ),
            out_shape=[
                jax.ShapeDtypeStruct((rows, width), jnp.float32),
                jax.ShapeDtypeStruct((rows, width), jnp.bfloat16),
                jax.ShapeDtypeStruct(pos.shape, jnp.float32),
            ],
            compiler_params=params,
            cost_estimate=pl.CostEstimate(
                flops=flops * 2, bytes_accessed=4000000, transcendentals=flops // 128
            ),
        )(*plan[:3], queries, key_values, pos, first)

    def backward(attended, log_total, grads):
        return pl.pallas_call(
            functools.partial(backward_kernel, key_len, head_dim ** (-0.5)),
            grid_spec=pltpu.PrefetchScalarGridSpec(
                num_scalar_prefetch=4,
                grid=(seq_count, 2),
                in_specs=[row_spec, kv_spec, lane_spec, lane_spec, row_spec, lane_spec, row_spec],
                out_specs=[row_spec, kv_spec],
                scratch_shapes=[
                    sorted_shape,
                    pltpu.VMEM((blocks * block_len, 2 * head_dim), jnp.float32),
                ],
            ),
            out_shape=[
                jax.ShapeDtypeStruct((rows, width), jnp.float32),
                jax.ShapeDtypeStruct(key_values.shape, jnp.bfloat16),
            ],
            compiler_params=params,
            cost_estimate=pl.CostEstimate(
                flops=flops * 5, bytes_accessed=8000000, transcendentals=flops // 128
            ),
        )(*plan, queries, key_values, pos, first, attended, log_total, grads)

    return forward, backward


def shards(
    tokens,
    attn_gain,
    w_query,
    b_query,
    w_key,
    b_key,
    w_value,
    b_value,
    w_out,
    mlp_gain,
    w_gate,
    w_up,
    w_down,
    cotangent,
    block_table,
    doc_lengths,
):
    tok_rows, model_width = tokens.shape
    head_dim = w_key.shape[1]
    group = w_query.shape[1] // head_dim
    seq_count = doc_lengths.shape[0]
    half_rows = tok_rows // seq_count
    block_len = half_rows // 2
    ctx_size = lax.axis_size("ctx")
    seq_len = ctx_size * half_rows
    scale = head_dim ** (-0.5)
    own_index = lax.axis_index("ctx")
    pair_blocks = jnp.stack([block_table, 2 * ctx_size - 1 - block_table], axis=1)
    all_pos = (
        pair_blocks[:, :, None] * block_len + jnp.arange(block_len, dtype=jnp.int32)[None, None, :]
    ).reshape(seq_len)
    own_pos = lax.dynamic_slice_in_dim(all_pos, own_index * half_rows, half_rows)
    bits = bit_list(ctx_size)
    masks = [0]
    for bit in reversed(bits):
        masks = masks + [m ^ bit for m in masks]
    slots = jnp.array(masks, jnp.int32) ^ own_index
    key_blocks = pair_blocks[slots].reshape(2 * ctx_size)
    block_ids = jnp.arange(2 * ctx_size, dtype=jnp.int32)
    block_slots = jnp.sum(
        jnp.where(key_blocks[None, :] == block_ids[:, None], block_ids[None, :], 0), axis=1
    ).astype(jnp.int32)
    bounds = jnp.cumsum(doc_lengths, axis=1)
    own_first = jnp.max(
        jnp.where(own_pos[None, :, None] >= bounds[:, None, :], bounds[:, None, :], 0), axis=2
    )
    cos_table, sin_table = rope_tables(own_pos, head_dim)
    key_len = min(KEY_BLOCK, seq_len)
    pos_blocks = jnp.broadcast_to(
        own_pos.reshape(1, 2, block_len), (seq_count, 2, block_len)
    ).reshape(2 * seq_count, block_len)
    first_blocks = own_first.reshape(2 * seq_count, block_len)
    plan = (
        block_slots,
        first_blocks[:, 0] // key_len,
        pos_blocks[:, -1] // key_len + 1,
        key_blocks,
    )
    lane_pos = jnp.tile(pos_blocks, (1, group))[:, None, :]
    lane_first = jnp.tile(first_blocks, (1, group))[:, None, :]
    x_float = tokens.astype(jnp.float32)
    gain_one = attn_gain.astype(jnp.float32)
    gain_two = mlp_gain.astype(jnp.float32)
    inv_one = lax.rsqrt(jnp.mean(x_float * x_float, axis=1, keepdims=True) + EPSILON)
    normed = (x_float * inv_one * gain_one).astype(jnp.bfloat16)
    query_pre = jnp.dot(normed, w_query, preferred_element_type=jnp.float32) + b_query.astype(
        jnp.float32
    )
    key_pre = jnp.dot(normed, w_key, preferred_element_type=jnp.float32) + b_key.astype(jnp.float32)
    value_rows = (
        jnp.dot(normed, w_value, preferred_element_type=jnp.float32) + b_value.astype(jnp.float32)
    ).astype(jnp.bfloat16)
    query_rot = rotate(
        query_pre.reshape(seq_count, half_rows, group, head_dim), cos_table, sin_table
    ).astype(jnp.bfloat16)
    query_low = (query_rot.astype(jnp.float32) * scale).astype(jnp.bfloat16).reshape(tok_rows, group * head_dim)
    key_local = (
        rotate(key_pre.reshape(seq_count, half_rows, 1, head_dim), cos_table, sin_table)
        .reshape(seq_count, half_rows, head_dim)
        .astype(jnp.bfloat16)
    )
    value_local = value_rows.reshape(seq_count, half_rows, head_dim)

    gathered = jnp.concatenate([key_local, value_local], axis=2)
    for bit in reversed(bits):
        gathered = jnp.concatenate([gathered, swap(gathered, "ctx", bit)], axis=1)
    key_values = gathered.reshape(seq_count, 2 * ctx_size, block_len, 2 * head_dim)
    attend, attend_back = attention(
        seq_count, key_len, head_dim, plan, query_low, key_values, lane_pos, lane_first
    )
    attended, attn_low, log_total = attend()
    branch = sum_pair(jnp.dot(attn_low, w_out, preferred_element_type=jnp.float32))
    stream = x_float + branch
    inv_two = lax.rsqrt(jnp.mean(stream * stream, axis=1, keepdims=True) + EPSILON)
    normed_two = (stream * inv_two * gain_two).astype(jnp.bfloat16)
    gate_pre = jnp.dot(normed_two, w_gate, preferred_element_type=jnp.float32)
    upward = jnp.dot(normed_two, w_up, preferred_element_type=jnp.float32)
    sigmoid_gate = jax.nn.sigmoid(gate_pre)
    swish = gate_pre * sigmoid_gate
    hidden = (swish * upward).astype(jnp.bfloat16)
    down_part = sum_pair(jnp.dot(hidden, w_down, preferred_element_type=jnp.float32))
    mixed = (stream + down_part).astype(jnp.bfloat16)
    grad_f = cotangent.astype(jnp.float32)
    grad_w_down = jnp.dot(cotangent.T, hidden, preferred_element_type=jnp.float32)
    grad_hidden = jnp.dot(cotangent, w_down.T, preferred_element_type=jnp.float32)
    grad_gate_low = (
        grad_hidden * upward * sigmoid_gate * (1.0 + gate_pre * (1.0 - sigmoid_gate))
    ).astype(jnp.bfloat16)
    grad_up_low = (grad_hidden * swish).astype(jnp.bfloat16)
    grad_w_gate = jnp.dot(normed_two.T, grad_gate_low, preferred_element_type=jnp.float32)
    grad_w_up = jnp.dot(normed_two.T, grad_up_low, preferred_element_type=jnp.float32)
    grad_normed_part = jnp.dot(
        grad_gate_low, w_gate.T, preferred_element_type=jnp.float32
    ) + jnp.dot(grad_up_low, w_up.T, preferred_element_type=jnp.float32)
    grad_normed_two = sum_pair(grad_normed_part)
    grad_stream_part, grad_mlp_gain = norm_back(grad_normed_two, stream, inv_two, gain_two)
    grad_stream = grad_f + grad_stream_part
    grad_branch = grad_stream.astype(jnp.bfloat16)
    grad_w_out = jnp.dot(grad_branch.T, attn_low, preferred_element_type=jnp.float32)
    grad_attn_low = jnp.dot(grad_branch, w_out.T, preferred_element_type=jnp.float32).astype(
        jnp.bfloat16
    )
    grad_query_rows, grad_key_values = attend_back(attended, log_total, grad_attn_low)
    cur = grad_key_values.reshape(seq_count, seq_len, 2 * head_dim)
    for bit in bits:
        half = cur.shape[1] // 2
        total = cur[:, :half].astype(jnp.float32) + swap(cur[:, half:], "ctx", bit).astype(
            jnp.float32
        )
        cur = total if bit == bits[-1] else total.astype(jnp.bfloat16)
    grad_keys_own = cur[:, :, :head_dim]
    grad_values_own = cur[:, :, head_dim:]
    grad_query_rows = grad_query_rows.reshape(seq_count, half_rows, group, head_dim)
    grad_query_low = (
        rotate(grad_query_rows, cos_table, -sin_table)
        .reshape(tok_rows, group * head_dim)
        .astype(jnp.bfloat16)
    )
    grad_key_low = (
        rotate(grad_keys_own.reshape(seq_count, half_rows, 1, head_dim), cos_table, -sin_table)
        .reshape(tok_rows, head_dim)
        .astype(jnp.bfloat16)
    )
    grad_value_low = grad_values_own.reshape(tok_rows, head_dim).astype(jnp.bfloat16)
    grad_w_query = jnp.dot(normed.T, grad_query_low, preferred_element_type=jnp.float32)
    grad_w_key = jnp.dot(normed.T, grad_key_low, preferred_element_type=jnp.float32)
    grad_w_value = jnp.dot(normed.T, grad_value_low, preferred_element_type=jnp.float32)
    grad_b_query = jnp.sum(grad_query_low.astype(jnp.float32), axis=0)
    grad_b_key = jnp.sum(grad_key_low.astype(jnp.float32), axis=0)
    grad_b_value = jnp.sum(grad_value_low.astype(jnp.float32), axis=0)
    grad_first_part = (
        jnp.dot(grad_query_low, w_query.T, preferred_element_type=jnp.float32)
        + jnp.dot(grad_key_low, w_key.T, preferred_element_type=jnp.float32)
        + jnp.dot(grad_value_low, w_value.T, preferred_element_type=jnp.float32)
    )
    grad_normed = sum_pair(grad_first_part)
    grad_in_part, grad_attn_gain = norm_back(grad_normed, x_float, inv_one, gain_one)
    grad_tokens = grad_stream + grad_in_part
    other = [bits[1], bits[0]] + bits[2:]

    def scatter(matrix, order):
        return scatter_rows(matrix.astype(jnp.bfloat16), order)

    last = bits[2:] + bits[:2]
    sum_down = scatter(grad_w_down, last).T
    sum_gate = scatter(grad_w_gate, bits)
    sum_up = scatter(grad_w_up, other)
    sum_out = scatter(grad_w_out, other).T
    sum_query = scatter(grad_w_query, bits)
    key_value_sum = scatter(jnp.concatenate([grad_w_key, grad_w_value], axis=1), other)
    sum_key = key_value_sum[:, :head_dim]
    sum_value = key_value_sum[:, head_dim:]
    pieces = (grad_attn_gain, grad_mlp_gain, grad_b_query, grad_b_key, grad_b_value)
    flat = jnp.concatenate(pieces)
    padded = -(-flat.shape[0] // 1024) * 1024
    flat = jnp.pad(flat, (0, padded - flat.shape[0])).reshape(8, padded // 8)
    for bit in bits:
        flat = flat + swap(flat, "ctx", bit)
    flat = flat.reshape(padded)
    small = []
    begin = 0
    for piece in pieces:
        small.append(flat[begin : begin + piece.shape[0]])
        begin += piece.shape[0]
    return (
        mixed,
        grad_tokens,
        small[0],
        sum_query,
        small[2],
        sum_key,
        small[3],
        sum_value,
        small[4],
        sum_out,
        small[1],
        sum_gate,
        sum_up,
        sum_down,
    )


def solution(mesh):
    return jax.shard_map(
        shards,
        mesh=mesh,
        in_specs=(
            P("ctx", None),
            P(),
            P(None, "tp"),
            P("tp"),
            P(None, "tp"),
            P("tp"),
            P(None, "tp"),
            P("tp"),
            P("tp", None),
            P(),
            P(None, "tp"),
            P(None, "tp"),
            P("tp", None),
            P("ctx", None),
            P(),
            P(),
        ),
        out_specs=(
            P("ctx", None),
            P("ctx", None),
            P(),
            P("ctx", "tp"),
            P("tp"),
            P("ctx", "tp"),
            P("tp"),
            P("ctx", "tp"),
            P("tp"),
            P("tp", "ctx"),
            P(),
            P("ctx", "tp"),
            P("ctx", "tp"),
            P("tp", "ctx"),
        ),
        check_vma=False,
    )
```

```python
import functools

import jax
import jax.numpy as jnp
from jax import lax
from jax.experimental import pallas as pl
from jax.experimental.pallas import tpu as pltpu
from jax.sharding import PartitionSpec as P

EPSILON = 1e-06
THETA = 1000000.0
NEGATIVE = -1e30
KEY_BLOCK = 256
VMEM_BYTES = 40 * 1024 * 1024
CONTRACT_LAST = (((1,), (1,)), ((), ()))
CONTRACT_FIRST = (((0,), (0,)), ((), ()))


def rope_tables(positions, head_width):
    half_width = head_width // 2
    frequency = THETA ** (-jnp.arange(half_width, dtype=jnp.float32) * 2.0 / head_width)
    angles = positions.astype(jnp.float32)[:, None] * frequency[None, :]
    return (jnp.cos(angles), jnp.sin(angles))


def rotate(values, cos_table, sin_table):
    half_width = values.shape[-1] // 2
    cos_part = cos_table[:, None, :]
    sin_part = sin_table[:, None, :]
    first_half = values[..., :half_width]
    second_half = values[..., half_width:]
    return jnp.concatenate(
        [
            first_half * cos_part - second_half * sin_part,
            second_half * cos_part + first_half * sin_part,
        ],
        axis=-1,
    )


def norm_back(grad_normed, inputs, inverse, gain_f):
    scaled = grad_normed * gain_f
    grad_in = inverse * scaled - inputs * (inverse * inverse * inverse) * jnp.mean(
        scaled * inputs, axis=1, keepdims=True
    )
    grad_gain = jnp.sum(grad_normed * inputs * inverse, axis=0)
    return (grad_in, grad_gain)


def swap(values, axis_name, bit):
    size = lax.axis_size(axis_name)
    return lax.ppermute(values, axis_name, [(i, i ^ bit) for i in range(size)])


def sum_pair(part):
    low = part.astype(jnp.bfloat16)
    return low.astype(jnp.float32) + swap(low, "tp", 1).astype(jnp.float32)


def bit_list(count):
    return [1 << b for b in range(count.bit_length() - 1)]


class RowScatter:
    def __init__(self, matrix, order):
        self.cur = matrix.astype(jnp.bfloat16)
        self.order = list(order)
        self.block = matrix.shape[0] // lax.axis_size("ctx")
        self.columns = matrix.shape[1]

    def stage(self):
        bit = self.order.pop(0)
        left = sorted(self.order + [bit], reverse=True)
        at = left.index(bit)
        before = 1 << at
        after = 1 << (len(left) - at - 1)
        shaped = self.cur.reshape(before, 2, after * self.block, self.columns)
        mine = (lax.axis_index("ctx") // bit) % 2
        keep = lax.dynamic_index_in_dim(shaped, mine, 1, keepdims=False)
        send = lax.dynamic_index_in_dim(shaped, 1 - mine, 1, keepdims=False)
        got = swap(send, "ctx", bit)
        total = keep.astype(jnp.float32) + got.astype(jnp.float32)
        total = total.reshape(before * after * self.block, self.columns)
        self.cur = total.astype(jnp.bfloat16) if self.order else total

    def finish(self):
        while self.order:
            self.stage()
        return self.cur


def in_step(flows, *others):
    held = lax.optimization_barrier(tuple(flow.cur for flow in flows) + others)
    for flow, cur in zip(flows, held):
        flow.cur = cur
    return held[len(flows) :]


def stack_heads(rows, head_dim):
    heads = rows.shape[1] // head_dim
    return jnp.concatenate(
        [rows[:, h * head_dim : (h + 1) * head_dim] for h in range(heads)], axis=0
    )


def unstack_heads(stacked, count):
    heads = stacked.shape[0] // count
    return jnp.concatenate([stacked[h * count : (h + 1) * count] for h in range(heads)], axis=1)


def sort_blocks(slot_ref, kv_ref, sorted_ref):
    blocks, block_len = kv_ref.shape[1], kv_ref.shape[2]

    def move(b, carry):
        sorted_ref[pl.ds(pl.multiple_of(b * block_len, block_len), block_len), :] = kv_ref[
            0, slot_ref[b]
        ]
        return carry

    lax.fori_loop(0, blocks, move, 0)


def forward_kernel(
    key_len, slot_ref, low_ref, high_ref, q_ref, kv_ref, pos_ref, first_ref,
    attn_ref, low_attn_ref, log_ref, sorted_ref,
):
    step = pl.program_id(0) * pl.num_programs(1) + pl.program_id(1)
    head_dim = kv_ref.shape[3] // 2
    count = q_ref.shape[0]

    @pl.when(pl.program_id(1) == 0)
    def _():
        sort_blocks(slot_ref, kv_ref, sorted_ref)

    queries = stack_heads(q_ref[...].astype(jnp.float32), head_dim).astype(jnp.bfloat16)
    rows = queries.shape[0]
    q_pos, q_first = pos_ref[0], first_ref[0]

    def body(j, carry):
        top, total, acc = carry
        start = pl.multiple_of(j * key_len, key_len)
        both = sorted_ref[pl.ds(start, key_len), :]
        keys, values = both[:, :head_dim], both[:, head_dim:]
        scores = lax.dot_general(keys, queries, CONTRACT_LAST, preferred_element_type=jnp.float32)
        k_pos = start + lax.broadcasted_iota(jnp.int32, scores.shape, 0)
        seen = (k_pos <= q_pos) & (k_pos >= q_first)
        scores = jnp.where(seen, scores, NEGATIVE)
        new_top = jnp.maximum(top, jnp.max(scores, axis=0, keepdims=True))
        weights = jnp.where(seen, jnp.exp(scores - new_top), 0.0)
        factor = jnp.exp(top - new_top)
        total = total * factor + jnp.sum(weights, axis=0, keepdims=True)
        acc = acc * factor + lax.dot_general(
            values, weights.astype(jnp.bfloat16), CONTRACT_FIRST,
            preferred_element_type=jnp.float32,
        )
        return new_top, total, acc

    init = (
        jnp.full((1, rows), NEGATIVE, jnp.float32),
        jnp.zeros((1, rows), jnp.float32),
        jnp.zeros((head_dim, rows), jnp.float32),
    )
    top, total, acc = lax.fori_loop(low_ref[step], high_ref[step], body, init)
    out = unstack_heads((acc / total).T, count)
    attn_ref[...] = out
    low_attn_ref[...] = out.astype(jnp.bfloat16)
    log_ref[0] = top + jnp.log(total)


def backward_kernel(
    key_len, scale, slot_ref, low_ref, high_ref, block_ref, q_ref, kv_ref, pos_ref, first_ref,
    attn_ref, log_ref, grad_ref, cos_ref, sin_ref, grad_q_ref, grad_kv_ref, sorted_ref, acc_ref,
):
    step = pl.program_id(0) * pl.num_programs(1) + pl.program_id(1)
    head_dim = kv_ref.shape[3] // 2
    blocks, block_len = kv_ref.shape[1], kv_ref.shape[2]
    count = q_ref.shape[0]

    @pl.when(pl.program_id(1) == 0)
    def _():
        sort_blocks(slot_ref, kv_ref, sorted_ref)
        acc_ref[...] = jnp.zeros_like(acc_ref)

    queries = stack_heads(q_ref[...].astype(jnp.float32), head_dim).astype(jnp.bfloat16)
    grad_f = grad_ref[...].astype(jnp.float32)
    grads = stack_heads(grad_f, head_dim).astype(jnp.bfloat16)
    delta = jnp.sum(stack_heads(grad_f * attn_ref[...], head_dim).T, axis=0, keepdims=True)
    rows = queries.shape[0]
    q_pos, q_first, log_total = pos_ref[0], first_ref[0], log_ref[0]

    def body(j, grad_q):
        start = pl.multiple_of(j * key_len, key_len)
        both = sorted_ref[pl.ds(start, key_len), :]
        keys, values = both[:, :head_dim], both[:, head_dim:]
        scores = lax.dot_general(keys, queries, CONTRACT_LAST, preferred_element_type=jnp.float32)
        k_pos = start + lax.broadcasted_iota(jnp.int32, scores.shape, 0)
        seen = (k_pos <= q_pos) & (k_pos >= q_first)
        shares = jnp.where(seen, jnp.exp(jnp.where(seen, scores - log_total, 0.0)), 0.0)
        grad_shares = lax.dot_general(
            values, grads, CONTRACT_LAST, preferred_element_type=jnp.float32
        )
        grad_scores = (shares * (grad_shares - delta)).astype(jnp.bfloat16)
        grad_values = jnp.dot(
            shares.astype(jnp.bfloat16), grads, preferred_element_type=jnp.float32
        )
        grad_keys = jnp.dot(grad_scores, queries, preferred_element_type=jnp.float32)
        acc_ref[pl.ds(start, key_len), :] += jnp.concatenate([grad_keys, grad_values], axis=1)
        return grad_q + lax.dot_general(
            keys, grad_scores, CONTRACT_FIRST, preferred_element_type=jnp.float32
        )

    grad_q = lax.fori_loop(
        low_ref[step], high_ref[step], body, jnp.zeros((head_dim, rows), jnp.float32)
    )
    half = head_dim // 2
    upper, lower = grad_q[:half] * scale, grad_q[half:] * scale
    cos_part, sin_part = cos_ref[0], sin_ref[0]
    turned = jnp.concatenate(
        [upper * cos_part + lower * sin_part, lower * cos_part - upper * sin_part], axis=0
    )
    grad_q_ref[...] = unstack_heads(turned.T, count).astype(jnp.bfloat16)

    @pl.when(pl.program_id(1) == pl.num_programs(1) - 1)
    def _():
        def move(k, carry):
            at = pl.multiple_of(block_ref[k] * block_len, block_len)
            grad_kv_ref[0, k] = acc_ref[pl.ds(at, block_len), :].astype(jnp.bfloat16)
            return carry

        lax.fori_loop(0, blocks, move, 0)


def attention(seq_count, key_len, head_dim, plan, queries, key_values, pos, first, turns):
    rows, width = queries.shape
    blocks, block_len = key_values.shape[1:3]
    stacked = pos.shape[2]
    row_spec = pl.BlockSpec((block_len, width), lambda s, j, *_: (s * 2 + j, 0))
    kv_spec = pl.BlockSpec((1, blocks, block_len, 2 * head_dim), lambda s, j, *_: (s, 0, 0, 0))
    lane_spec = pl.BlockSpec((1, 1, stacked), lambda s, j, *_: (s * 2 + j, 0, 0))
    turn_spec = pl.BlockSpec((1, head_dim // 2, stacked), lambda s, j, *_: (j, 0, 0))
    flops = 2 * 2 * rows * width * blocks * block_len // 2
    sorted_shape = pltpu.VMEM((blocks * block_len, 2 * head_dim), jnp.bfloat16)
    params = pltpu.CompilerParams(vmem_limit_bytes=VMEM_BYTES)

    def forward():
        return pl.pallas_call(
            functools.partial(forward_kernel, key_len),
            grid_spec=pltpu.PrefetchScalarGridSpec(
                num_scalar_prefetch=3,
                grid=(seq_count, 2),
                in_specs=[row_spec, kv_spec, lane_spec, lane_spec],
                out_specs=[row_spec, row_spec, lane_spec],
                scratch_shapes=[sorted_shape],
            ),
            out_shape=[
                jax.ShapeDtypeStruct((rows, width), jnp.float32),
                jax.ShapeDtypeStruct((rows, width), jnp.bfloat16),
                jax.ShapeDtypeStruct(pos.shape, jnp.float32),
            ],
            compiler_params=params,
            cost_estimate=pl.CostEstimate(
                flops=flops * 2, bytes_accessed=4000000, transcendentals=flops // 128
            ),
        )(*plan[:3], queries, key_values, pos, first)

    def backward(attended, log_total, grads):
        return pl.pallas_call(
            functools.partial(backward_kernel, key_len, head_dim ** (-0.5)),
            grid_spec=pltpu.PrefetchScalarGridSpec(
                num_scalar_prefetch=4,
                grid=(seq_count, 2),
                in_specs=[row_spec, kv_spec, lane_spec, lane_spec, row_spec, lane_spec, row_spec,
                          turn_spec, turn_spec],
                out_specs=[row_spec, kv_spec],
                scratch_shapes=[
                    sorted_shape,
                    pltpu.VMEM((blocks * block_len, 2 * head_dim), jnp.float32),
                ],
            ),
            out_shape=[
                jax.ShapeDtypeStruct((rows, width), jnp.bfloat16),
                jax.ShapeDtypeStruct(key_values.shape, jnp.bfloat16),
            ],
            compiler_params=params,
            cost_estimate=pl.CostEstimate(
                flops=flops * 5, bytes_accessed=8000000, transcendentals=flops // 128
            ),
        )(*plan, queries, key_values, pos, first, attended, log_total, grads, *turns)

    return forward, backward


def shards(
    tokens,
    attn_gain,
    w_query,
    b_query,
    w_key,
    b_key,
    w_value,
    b_value,
    w_out,
    mlp_gain,
    w_gate,
    w_up,
    w_down,
    cotangent,
    block_table,
    doc_lengths,
):
    tok_rows, model_width = tokens.shape
    head_dim = w_key.shape[1]
    group = w_query.shape[1] // head_dim
    seq_count = doc_lengths.shape[0]
    half_rows = tok_rows // seq_count
    block_len = half_rows // 2
    ctx_size = lax.axis_size("ctx")
    seq_len = ctx_size * half_rows
    scale = head_dim ** (-0.5)
    own_index = lax.axis_index("ctx")
    pair_blocks = jnp.stack([block_table, 2 * ctx_size - 1 - block_table], axis=1)
    all_pos = (
        pair_blocks[:, :, None] * block_len + jnp.arange(block_len, dtype=jnp.int32)[None, None, :]
    ).reshape(seq_len)
    own_pos = lax.dynamic_slice_in_dim(all_pos, own_index * half_rows, half_rows)
    bits = bit_list(ctx_size)
    masks = [0]
    for bit in reversed(bits):
        masks = masks + [m ^ bit for m in masks]
    slots = jnp.array(masks, jnp.int32) ^ own_index
    key_blocks = pair_blocks[slots].reshape(2 * ctx_size)
    block_ids = jnp.arange(2 * ctx_size, dtype=jnp.int32)
    block_slots = jnp.sum(
        jnp.where(key_blocks[None, :] == block_ids[:, None], block_ids[None, :], 0), axis=1
    ).astype(jnp.int32)
    bounds = jnp.cumsum(doc_lengths, axis=1)
    own_first = jnp.max(
        jnp.where(own_pos[None, :, None] >= bounds[:, None, :], bounds[:, None, :], 0), axis=2
    )
    cos_table, sin_table = rope_tables(own_pos, head_dim)
    key_len = min(KEY_BLOCK, seq_len)
    pos_blocks = jnp.broadcast_to(
        own_pos.reshape(1, 2, block_len), (seq_count, 2, block_len)
    ).reshape(2 * seq_count, block_len)
    first_blocks = own_first.reshape(2 * seq_count, block_len)
    turns = [
        jnp.tile(table.reshape(2, block_len, head_dim // 2).transpose(0, 2, 1), (1, 1, group))
        for table in (cos_table, sin_table)
    ]
    plan = (
        block_slots,
        first_blocks[:, 0] // key_len,
        pos_blocks[:, -1] // key_len + 1,
        key_blocks,
    )
    lane_pos = jnp.tile(pos_blocks, (1, group))[:, None, :]
    lane_first = jnp.tile(first_blocks, (1, group))[:, None, :]
    x_float = tokens.astype(jnp.float32)
    gain_one = attn_gain.astype(jnp.float32)
    gain_two = mlp_gain.astype(jnp.float32)
    inv_one = lax.rsqrt(jnp.mean(x_float * x_float, axis=1, keepdims=True) + EPSILON)
    normed = (x_float * inv_one * gain_one).astype(jnp.bfloat16)
    query_pre = jnp.dot(normed, w_query, preferred_element_type=jnp.float32) + b_query.astype(
        jnp.float32
    )
    key_pre = jnp.dot(normed, w_key, preferred_element_type=jnp.float32) + b_key.astype(jnp.float32)
    value_rows = (
        jnp.dot(normed, w_value, preferred_element_type=jnp.float32) + b_value.astype(jnp.float32)
    ).astype(jnp.bfloat16)
    query_rot = rotate(
        query_pre.reshape(seq_count, half_rows, group, head_dim), cos_table, sin_table
    ).astype(jnp.bfloat16)
    query_low = (query_rot.astype(jnp.float32) * scale).astype(jnp.bfloat16).reshape(tok_rows, group * head_dim)
    key_local = (
        rotate(key_pre.reshape(seq_count, half_rows, 1, head_dim), cos_table, sin_table)
        .reshape(seq_count, half_rows, head_dim)
        .astype(jnp.bfloat16)
    )
    value_local = value_rows.reshape(seq_count, half_rows, head_dim)

    gathered = jnp.concatenate([key_local, value_local], axis=2)
    for bit in reversed(bits):
        gathered = jnp.concatenate([gathered, swap(gathered, "ctx", bit)], axis=1)
    key_values = gathered.reshape(seq_count, 2 * ctx_size, block_len, 2 * head_dim)
    attend, attend_back = attention(
        seq_count, key_len, head_dim, plan, query_low, key_values, lane_pos, lane_first, turns
    )
    attended, attn_low, log_total = attend()
    branch = sum_pair(jnp.dot(attn_low, w_out, preferred_element_type=jnp.float32))
    stream = x_float + branch
    inv_two = lax.rsqrt(jnp.mean(stream * stream, axis=1, keepdims=True) + EPSILON)
    normed_two = (stream * inv_two * gain_two).astype(jnp.bfloat16)
    gate_pre = jnp.dot(normed_two, w_gate, preferred_element_type=jnp.float32)
    upward = jnp.dot(normed_two, w_up, preferred_element_type=jnp.float32)
    sigmoid_gate = jax.nn.sigmoid(gate_pre)
    swish = gate_pre * sigmoid_gate
    hidden = (swish * upward).astype(jnp.bfloat16)
    down_part = sum_pair(jnp.dot(hidden, w_down, preferred_element_type=jnp.float32))
    mixed = (stream + down_part).astype(jnp.bfloat16)
    grad_f = cotangent.astype(jnp.float32)
    grad_w_down = jnp.dot(cotangent.T, hidden, preferred_element_type=jnp.float32)
    grad_hidden = jnp.dot(cotangent, w_down.T, preferred_element_type=jnp.float32)
    grad_gate_low = (
        grad_hidden * upward * sigmoid_gate * (1.0 + gate_pre * (1.0 - sigmoid_gate))
    ).astype(jnp.bfloat16)
    grad_up_low = (grad_hidden * swish).astype(jnp.bfloat16)
    grad_w_gate = jnp.dot(normed_two.T, grad_gate_low, preferred_element_type=jnp.float32)
    grad_w_up = jnp.dot(normed_two.T, grad_up_low, preferred_element_type=jnp.float32)
    grad_normed_part = jnp.dot(
        grad_gate_low, w_gate.T, preferred_element_type=jnp.float32
    ) + jnp.dot(grad_up_low, w_up.T, preferred_element_type=jnp.float32)
    grad_normed_two = sum_pair(grad_normed_part)
    grad_stream_part, grad_mlp_gain = norm_back(grad_normed_two, stream, inv_two, gain_two)
    grad_stream = grad_f + grad_stream_part
    grad_branch = grad_stream.astype(jnp.bfloat16)
    grad_w_out = jnp.dot(grad_branch.T, attn_low, preferred_element_type=jnp.float32)
    grad_attn_low = jnp.dot(grad_branch, w_out.T, preferred_element_type=jnp.float32).astype(
        jnp.bfloat16
    )
    other = [bits[1], bits[0]] + bits[2:]
    last = bits[2:] + bits[:2]
    flow_down = RowScatter(grad_w_down, last)
    flow_gate = RowScatter(grad_w_gate, bits)
    flow_up = RowScatter(grad_w_up, other)
    flow_out = RowScatter(grad_w_out, other)
    flows = [flow_down, flow_gate, flow_up, flow_out]
    for flow in flows:
        flow.stage()
    grad_query_low, grad_key_values = attend_back(attended, log_total, grad_attn_low)
    cur = grad_key_values.reshape(seq_count, seq_len, 2 * head_dim)
    for bit in bits:
        half = cur.shape[1] // 2
        total = cur[:, :half].astype(jnp.float32) + swap(cur[:, half:], "ctx", bit).astype(
            jnp.float32
        )
        cur = total if bit == bits[-1] else total.astype(jnp.bfloat16)
        if bit == bits[0]:
            (cur,) = in_step(flows, cur)
            for flow in flows:
                flow.stage()
    grad_keys_own = cur[:, :, :head_dim]
    grad_values_own = cur[:, :, head_dim:]
    flow_query = RowScatter(
        jnp.dot(normed.T, grad_query_low, preferred_element_type=jnp.float32), bits
    )
    flow_query.stage()
    flow_query.stage()
    grad_key_low = (
        rotate(grad_keys_own.reshape(seq_count, half_rows, 1, head_dim), cos_table, -sin_table)
        .reshape(tok_rows, head_dim)
        .astype(jnp.bfloat16)
    )
    grad_value_low = grad_values_own.reshape(tok_rows, head_dim).astype(jnp.bfloat16)
    grad_w_key = jnp.dot(normed.T, grad_key_low, preferred_element_type=jnp.float32)
    grad_w_value = jnp.dot(normed.T, grad_value_low, preferred_element_type=jnp.float32)
    grad_b_query = jnp.sum(grad_query_low.astype(jnp.float32), axis=0)
    grad_b_key = jnp.sum(grad_key_low.astype(jnp.float32), axis=0)
    grad_b_value = jnp.sum(grad_value_low.astype(jnp.float32), axis=0)
    grad_first_part = (
        jnp.dot(grad_query_low, w_query.T, preferred_element_type=jnp.float32)
        + jnp.dot(grad_key_low, w_key.T, preferred_element_type=jnp.float32)
        + jnp.dot(grad_value_low, w_value.T, preferred_element_type=jnp.float32)
    )
    flows = flows + [flow_query]
    grad_w_pair = jnp.concatenate([grad_w_key, grad_w_value], axis=1).astype(jnp.bfloat16)
    first_low, grad_w_pair = in_step(
        flows, grad_first_part.astype(jnp.bfloat16), grad_w_pair
    )
    for flow in flows:
        flow.stage()
    flow_pair = RowScatter(grad_w_pair, other)
    flow_pair.stage()
    flow_pair.stage()
    grad_normed = sum_pair(first_low)
    grad_in_part, grad_attn_gain = norm_back(grad_normed, x_float, inv_one, gain_one)
    grad_tokens = grad_stream + grad_in_part
    in_step(flows + [flow_pair])
    sum_down = flow_down.finish().T
    sum_gate = flow_gate.finish()
    sum_up = flow_up.finish()
    sum_out = flow_out.finish().T
    sum_query = flow_query.finish()
    key_value_sum = flow_pair.finish()
    sum_key = key_value_sum[:, :head_dim]
    sum_value = key_value_sum[:, head_dim:]
    pieces = (grad_attn_gain, grad_mlp_gain, grad_b_query, grad_b_key, grad_b_value)
    flat = jnp.concatenate(pieces)
    padded = -(-flat.shape[0] // 1024) * 1024
    flat = jnp.pad(flat, (0, padded - flat.shape[0])).reshape(8, padded // 8)
    for bit in bits:
        flat = flat + swap(flat, "ctx", bit)
    flat = flat.reshape(padded)
    small = []
    begin = 0
    for piece in pieces:
        small.append(flat[begin : begin + piece.shape[0]])
        begin += piece.shape[0]
    return (
        mixed,
        grad_tokens,
        small[0],
        sum_query,
        small[2],
        sum_key,
        small[3],
        sum_value,
        small[4],
        sum_out,
        small[1],
        sum_gate,
        sum_up,
        sum_down,
    )


def solution(mesh):
    return jax.shard_map(
        shards,
        mesh=mesh,
        in_specs=(
            P("ctx", None),
            P(),
            P(None, "tp"),
            P("tp"),
            P(None, "tp"),
            P("tp"),
            P(None, "tp"),
            P("tp"),
            P("tp", None),
            P(),
            P(None, "tp"),
            P(None, "tp"),
            P("tp", None),
            P("ctx", None),
            P(),
            P(),
        ),
        out_specs=(
            P("ctx", None),
            P("ctx", None),
            P(),
            P("ctx", "tp"),
            P("tp"),
            P("ctx", "tp"),
            P("tp"),
            P("ctx", "tp"),
            P("tp"),
            P("tp", "ctx"),
            P(),
            P("ctx", "tp"),
            P("ctx", "tp"),
            P("tp", "ctx"),
        ),
        check_vma=False,
    )
```

```python
import functools

import jax
import jax.numpy as jnp
from jax import lax
from jax.experimental import pallas as pl
from jax.experimental.pallas import tpu as pltpu
from jax.sharding import PartitionSpec as P

EPSILON = 1e-06
THETA = 1000000.0
NEGATIVE = -1e30
KEY_BLOCK = 256
VMEM_BYTES = 40 * 1024 * 1024
CONTRACT_LAST = (((1,), (1,)), ((), ()))
CONTRACT_FIRST = (((0,), (0,)), ((), ()))


def rope_tables(positions, head_width):
    half_width = head_width // 2
    frequency = THETA ** (-jnp.arange(half_width, dtype=jnp.float32) * 2.0 / head_width)
    angles = positions.astype(jnp.float32)[:, None] * frequency[None, :]
    return (jnp.cos(angles), jnp.sin(angles))


def rotate(values, cos_table, sin_table):
    half_width = values.shape[-1] // 2
    cos_part = cos_table[:, None, :]
    sin_part = sin_table[:, None, :]
    first_half = values[..., :half_width]
    second_half = values[..., half_width:]
    return jnp.concatenate(
        [
            first_half * cos_part - second_half * sin_part,
            second_half * cos_part + first_half * sin_part,
        ],
        axis=-1,
    )


def norm_back(grad_normed, inputs, inverse, gain_f):
    scaled = grad_normed * gain_f
    grad_in = inverse * scaled - inputs * (inverse * inverse * inverse) * jnp.mean(
        scaled * inputs, axis=1, keepdims=True
    )
    grad_gain = jnp.sum(grad_normed * inputs * inverse, axis=0)
    return (grad_in, grad_gain)


def swap(values, axis_name, bit):
    size = lax.axis_size(axis_name)
    return lax.ppermute(values, axis_name, [(i, i ^ bit) for i in range(size)])


def sum_pair(part):
    low = part.astype(jnp.bfloat16)
    return low.astype(jnp.float32) + swap(low, "tp", 1).astype(jnp.float32)


def bit_list(count):
    return [1 << b for b in range(count.bit_length() - 1)]


class RowScatter:
    def __init__(self, matrix, order):
        self.cur = matrix.astype(jnp.bfloat16)
        self.order = list(order)
        self.block = matrix.shape[0] // lax.axis_size("ctx")
        self.columns = matrix.shape[1]

    def stage(self):
        bit = self.order.pop(0)
        left = sorted(self.order + [bit], reverse=True)
        at = left.index(bit)
        before = 1 << at
        after = 1 << (len(left) - at - 1)
        shaped = self.cur.reshape(before, 2, after * self.block, self.columns)
        mine = (lax.axis_index("ctx") // bit) % 2
        keep = lax.dynamic_index_in_dim(shaped, mine, 1, keepdims=False)
        send = lax.dynamic_index_in_dim(shaped, 1 - mine, 1, keepdims=False)
        got = swap(send, "ctx", bit)
        total = keep.astype(jnp.float32) + got.astype(jnp.float32)
        total = total.reshape(before * after * self.block, self.columns)
        self.cur = total.astype(jnp.bfloat16) if self.order else total

    def finish(self):
        while self.order:
            self.stage()
        return self.cur


def in_step(flows, *others):
    held = lax.optimization_barrier(tuple(flow.cur for flow in flows) + others)
    for flow, cur in zip(flows, held):
        flow.cur = cur
    return held[len(flows) :]


def stack_heads(rows, head_dim):
    heads = rows.shape[1] // head_dim
    return jnp.concatenate(
        [rows[:, h * head_dim : (h + 1) * head_dim] for h in range(heads)], axis=0
    )


def unstack_heads(stacked, count):
    heads = stacked.shape[0] // count
    return jnp.concatenate([stacked[h * count : (h + 1) * count] for h in range(heads)], axis=1)


def sort_blocks(slot_ref, kv_ref, sorted_ref):
    blocks, block_len = kv_ref.shape[1], kv_ref.shape[2]

    def move(b, carry):
        sorted_ref[pl.ds(pl.multiple_of(b * block_len, block_len), block_len), :] = kv_ref[
            0, slot_ref[b]
        ]
        return carry

    lax.fori_loop(0, blocks, move, 0)


def forward_kernel(
    key_len, slot_ref, low_ref, high_ref, q_ref, kv_ref, pos_ref, first_ref,
    attn_ref, low_attn_ref, log_ref, sorted_ref,
):
    step = pl.program_id(0) * pl.num_programs(1) + pl.program_id(1)
    head_dim = kv_ref.shape[3] // 2
    count = q_ref.shape[0]

    @pl.when(pl.program_id(1) == 0)
    def _():
        sort_blocks(slot_ref, kv_ref, sorted_ref)

    queries = stack_heads(q_ref[...].astype(jnp.float32), head_dim).astype(jnp.bfloat16)
    rows = queries.shape[0]
    q_pos, q_first = pos_ref[0], first_ref[0]

    def body(j, carry):
        top, total, acc = carry
        start = pl.multiple_of(j * key_len, key_len)
        both = sorted_ref[pl.ds(start, key_len), :]
        keys, values = both[:, :head_dim], both[:, head_dim:]
        scores = lax.dot_general(keys, queries, CONTRACT_LAST, preferred_element_type=jnp.float32)
        k_pos = start + lax.broadcasted_iota(jnp.int32, scores.shape, 0)
        seen = (k_pos <= q_pos) & (k_pos >= q_first)
        scores = jnp.where(seen, scores, NEGATIVE)
        new_top = jnp.maximum(top, jnp.max(scores, axis=0, keepdims=True))
        weights = jnp.where(seen, jnp.exp(scores - new_top), 0.0)
        factor = jnp.exp(top - new_top)
        total = total * factor + jnp.sum(weights, axis=0, keepdims=True)
        acc = acc * factor + lax.dot_general(
            values, weights.astype(jnp.bfloat16), CONTRACT_FIRST,
            preferred_element_type=jnp.float32,
        )
        return new_top, total, acc

    init = (
        jnp.full((1, rows), NEGATIVE, jnp.float32),
        jnp.zeros((1, rows), jnp.float32),
        jnp.zeros((head_dim, rows), jnp.float32),
    )
    top, total, acc = lax.fori_loop(low_ref[step], high_ref[step], body, init)
    out = unstack_heads((acc / total).T, count)
    attn_ref[...] = out
    low_attn_ref[...] = out.astype(jnp.bfloat16)
    log_ref[0] = top + jnp.log(total)


def backward_kernel(
    key_len, scale, slot_ref, low_ref, high_ref, block_ref, q_ref, kv_ref, pos_ref, first_ref,
    attn_ref, log_ref, grad_ref, cos_ref, sin_ref, grad_q_ref, grad_kv_ref, sorted_ref, acc_ref,
):
    step = pl.program_id(0) * pl.num_programs(1) + pl.program_id(1)
    head_dim = kv_ref.shape[3] // 2
    blocks, block_len = kv_ref.shape[1], kv_ref.shape[2]
    count = q_ref.shape[0]

    @pl.when(pl.program_id(1) == 0)
    def _():
        sort_blocks(slot_ref, kv_ref, sorted_ref)
        acc_ref[...] = jnp.zeros_like(acc_ref)

    queries = stack_heads(q_ref[...].astype(jnp.float32), head_dim).astype(jnp.bfloat16)
    grad_f = grad_ref[...].astype(jnp.float32)
    grads = stack_heads(grad_f, head_dim).astype(jnp.bfloat16)
    delta = jnp.sum(stack_heads(grad_f * attn_ref[...], head_dim).T, axis=0, keepdims=True)
    rows = queries.shape[0]
    q_pos, q_first, log_total = pos_ref[0], first_ref[0], log_ref[0]

    def body(j, grad_q):
        start = pl.multiple_of(j * key_len, key_len)
        both = sorted_ref[pl.ds(start, key_len), :]
        keys, values = both[:, :head_dim], both[:, head_dim:]
        scores = lax.dot_general(keys, queries, CONTRACT_LAST, preferred_element_type=jnp.float32)
        k_pos = start + lax.broadcasted_iota(jnp.int32, scores.shape, 0)
        seen = (k_pos <= q_pos) & (k_pos >= q_first)
        shares = jnp.where(seen, jnp.exp(jnp.where(seen, scores - log_total, 0.0)), 0.0)
        grad_shares = lax.dot_general(
            values, grads, CONTRACT_LAST, preferred_element_type=jnp.float32
        )
        grad_scores = (shares * (grad_shares - delta)).astype(jnp.bfloat16)
        grad_values = jnp.dot(
            shares.astype(jnp.bfloat16), grads, preferred_element_type=jnp.float32
        )
        grad_keys = jnp.dot(grad_scores, queries, preferred_element_type=jnp.float32)
        acc_ref[pl.ds(start, key_len), :] += jnp.concatenate([grad_keys, grad_values], axis=1)
        return grad_q + lax.dot_general(
            keys, grad_scores, CONTRACT_FIRST, preferred_element_type=jnp.float32
        )

    grad_q = lax.fori_loop(
        low_ref[step], high_ref[step], body, jnp.zeros((head_dim, rows), jnp.float32)
    )
    half = head_dim // 2
    upper, lower = grad_q[:half] * scale, grad_q[half:] * scale
    cos_part, sin_part = cos_ref[0], sin_ref[0]
    turned = jnp.concatenate(
        [upper * cos_part + lower * sin_part, lower * cos_part - upper * sin_part], axis=0
    )
    grad_q_ref[...] = unstack_heads(turned.T, count).astype(jnp.bfloat16)

    @pl.when(pl.program_id(1) == pl.num_programs(1) - 1)
    def _():
        def move(k, carry):
            at = pl.multiple_of(block_ref[k] * block_len, block_len)
            grad_kv_ref[0, k] = acc_ref[pl.ds(at, block_len), :].astype(jnp.bfloat16)
            return carry

        lax.fori_loop(0, blocks, move, 0)


def attention(seq_count, key_len, head_dim, plan, queries, key_values, pos, first, turns):
    rows, width = queries.shape
    blocks, block_len = key_values.shape[1:3]
    stacked = pos.shape[2]
    row_spec = pl.BlockSpec((block_len, width), lambda s, j, *_: (s * 2 + j, 0))
    kv_spec = pl.BlockSpec((1, blocks, block_len, 2 * head_dim), lambda s, j, *_: (s, 0, 0, 0))
    lane_spec = pl.BlockSpec((1, 1, stacked), lambda s, j, *_: (s * 2 + j, 0, 0))
    turn_spec = pl.BlockSpec((1, head_dim // 2, stacked), lambda s, j, *_: (j, 0, 0))
    flops = 2 * 2 * rows * width * blocks * block_len // 2
    sorted_shape = pltpu.VMEM((blocks * block_len, 2 * head_dim), jnp.bfloat16)
    params = pltpu.CompilerParams(vmem_limit_bytes=VMEM_BYTES)

    def forward():
        return pl.pallas_call(
            functools.partial(forward_kernel, key_len),
            grid_spec=pltpu.PrefetchScalarGridSpec(
                num_scalar_prefetch=3,
                grid=(seq_count, 2),
                in_specs=[row_spec, kv_spec, lane_spec, lane_spec],
                out_specs=[row_spec, row_spec, lane_spec],
                scratch_shapes=[sorted_shape],
            ),
            out_shape=[
                jax.ShapeDtypeStruct((rows, width), jnp.float32),
                jax.ShapeDtypeStruct((rows, width), jnp.bfloat16),
                jax.ShapeDtypeStruct(pos.shape, jnp.float32),
            ],
            compiler_params=params,
            cost_estimate=pl.CostEstimate(
                flops=flops * 2, bytes_accessed=4000000, transcendentals=flops // 128
            ),
        )(*plan[:3], queries, key_values, pos, first)

    def backward(attended, log_total, grads):
        return pl.pallas_call(
            functools.partial(backward_kernel, key_len, head_dim ** (-0.5)),
            grid_spec=pltpu.PrefetchScalarGridSpec(
                num_scalar_prefetch=4,
                grid=(seq_count, 2),
                in_specs=[row_spec, kv_spec, lane_spec, lane_spec, row_spec, lane_spec, row_spec,
                          turn_spec, turn_spec],
                out_specs=[row_spec, kv_spec],
                scratch_shapes=[
                    sorted_shape,
                    pltpu.VMEM((blocks * block_len, 2 * head_dim), jnp.float32),
                ],
            ),
            out_shape=[
                jax.ShapeDtypeStruct((rows, width), jnp.bfloat16),
                jax.ShapeDtypeStruct(key_values.shape, jnp.bfloat16),
            ],
            compiler_params=params,
            cost_estimate=pl.CostEstimate(
                flops=flops * 5, bytes_accessed=8000000, transcendentals=flops // 128
            ),
        )(*plan, queries, key_values, pos, first, attended, log_total, grads, *turns)

    return forward, backward


def shards(
    tokens,
    attn_gain,
    w_query,
    b_query,
    w_key,
    b_key,
    w_value,
    b_value,
    w_out,
    mlp_gain,
    w_gate,
    w_up,
    w_down,
    cotangent,
    block_table,
    doc_lengths,
):
    tok_rows, model_width = tokens.shape
    head_dim = w_key.shape[1]
    group = w_query.shape[1] // head_dim
    seq_count = doc_lengths.shape[0]
    half_rows = tok_rows // seq_count
    block_len = half_rows // 2
    ctx_size = lax.axis_size("ctx")
    seq_len = ctx_size * half_rows
    scale = head_dim ** (-0.5)
    own_index = lax.axis_index("ctx")
    pair_blocks = jnp.stack([block_table, 2 * ctx_size - 1 - block_table], axis=1)
    all_pos = (
        pair_blocks[:, :, None] * block_len + jnp.arange(block_len, dtype=jnp.int32)[None, None, :]
    ).reshape(seq_len)
    own_pos = lax.dynamic_slice_in_dim(all_pos, own_index * half_rows, half_rows)
    bits = bit_list(ctx_size)
    masks = [0]
    for bit in reversed(bits):
        masks = masks + [m ^ bit for m in masks]
    slots = jnp.array(masks, jnp.int32) ^ own_index
    key_blocks = pair_blocks[slots].reshape(2 * ctx_size)
    block_ids = jnp.arange(2 * ctx_size, dtype=jnp.int32)
    block_slots = jnp.sum(
        jnp.where(key_blocks[None, :] == block_ids[:, None], block_ids[None, :], 0), axis=1
    ).astype(jnp.int32)
    bounds = jnp.cumsum(doc_lengths, axis=1)
    own_first = jnp.max(
        jnp.where(own_pos[None, :, None] >= bounds[:, None, :], bounds[:, None, :], 0), axis=2
    )
    cos_table, sin_table = rope_tables(own_pos, head_dim)
    key_len = min(KEY_BLOCK, seq_len)
    pos_blocks = jnp.broadcast_to(
        own_pos.reshape(1, 2, block_len), (seq_count, 2, block_len)
    ).reshape(2 * seq_count, block_len)
    first_blocks = own_first.reshape(2 * seq_count, block_len)
    turns = [
        jnp.tile(table.reshape(2, block_len, head_dim // 2).transpose(0, 2, 1), (1, 1, group))
        for table in (cos_table, sin_table)
    ]
    plan = (
        block_slots,
        first_blocks[:, 0] // key_len,
        pos_blocks[:, -1] // key_len + 1,
        key_blocks,
    )
    lane_pos = jnp.tile(pos_blocks, (1, group))[:, None, :]
    lane_first = jnp.tile(first_blocks, (1, group))[:, None, :]
    x_float = tokens.astype(jnp.float32)
    gain_one = attn_gain.astype(jnp.float32)
    gain_two = mlp_gain.astype(jnp.float32)
    inv_one = lax.rsqrt(jnp.mean(x_float * x_float, axis=1, keepdims=True) + EPSILON)
    normed = (x_float * inv_one * gain_one).astype(jnp.bfloat16)
    query_pre = jnp.dot(normed, w_query, preferred_element_type=jnp.float32) + b_query.astype(
        jnp.float32
    )
    key_pre = jnp.dot(normed, w_key, preferred_element_type=jnp.float32) + b_key.astype(jnp.float32)
    value_rows = (
        jnp.dot(normed, w_value, preferred_element_type=jnp.float32) + b_value.astype(jnp.float32)
    ).astype(jnp.bfloat16)
    query_rot = rotate(
        query_pre.reshape(seq_count, half_rows, group, head_dim), cos_table, sin_table
    ).astype(jnp.bfloat16)
    query_low = (query_rot.astype(jnp.float32) * scale).astype(jnp.bfloat16).reshape(tok_rows, group * head_dim)
    key_local = (
        rotate(key_pre.reshape(seq_count, half_rows, 1, head_dim), cos_table, sin_table)
        .reshape(seq_count, half_rows, head_dim)
        .astype(jnp.bfloat16)
    )
    value_local = value_rows.reshape(seq_count, half_rows, head_dim)

    gathered = jnp.concatenate([key_local, value_local], axis=2)
    for bit in reversed(bits):
        gathered = jnp.concatenate([gathered, swap(gathered, "ctx", bit)], axis=1)
    key_values = gathered.reshape(seq_count, 2 * ctx_size, block_len, 2 * head_dim)
    attend, attend_back = attention(
        seq_count, key_len, head_dim, plan, query_low, key_values, lane_pos, lane_first, turns
    )
    attended, attn_low, log_total = attend()
    branch = sum_pair(jnp.dot(attn_low, w_out, preferred_element_type=jnp.float32))
    stream = x_float + branch
    inv_two = lax.rsqrt(jnp.mean(stream * stream, axis=1, keepdims=True) + EPSILON)
    normed_two = (stream * inv_two * gain_two).astype(jnp.bfloat16)
    gate_pre = jnp.dot(normed_two, w_gate, preferred_element_type=jnp.float32)
    upward = jnp.dot(normed_two, w_up, preferred_element_type=jnp.float32)
    sigmoid_gate = jax.nn.sigmoid(gate_pre)
    swish = gate_pre * sigmoid_gate
    hidden = (swish * upward).astype(jnp.bfloat16)
    down_part = sum_pair(jnp.dot(hidden, w_down, preferred_element_type=jnp.float32))
    mixed = (stream + down_part).astype(jnp.bfloat16)
    grad_f = cotangent.astype(jnp.float32)
    grad_w_down = jnp.dot(cotangent.T, hidden, preferred_element_type=jnp.float32)
    grad_hidden = jnp.dot(cotangent, w_down.T, preferred_element_type=jnp.float32)
    grad_gate_low = (
        grad_hidden * upward * sigmoid_gate * (1.0 + gate_pre * (1.0 - sigmoid_gate))
    ).astype(jnp.bfloat16)
    grad_up_low = (grad_hidden * swish).astype(jnp.bfloat16)
    grad_w_gate = jnp.dot(normed_two.T, grad_gate_low, preferred_element_type=jnp.float32)
    grad_w_up = jnp.dot(normed_two.T, grad_up_low, preferred_element_type=jnp.float32)
    grad_normed_part = jnp.dot(
        grad_gate_low, w_gate.T, preferred_element_type=jnp.float32
    ) + jnp.dot(grad_up_low, w_up.T, preferred_element_type=jnp.float32)
    grad_normed_two = sum_pair(grad_normed_part)
    grad_stream_part, grad_mlp_gain = norm_back(grad_normed_two, stream, inv_two, gain_two)
    grad_stream = grad_f + grad_stream_part
    grad_branch = grad_stream.astype(jnp.bfloat16)
    grad_w_out = jnp.dot(grad_branch.T, attn_low, preferred_element_type=jnp.float32)
    grad_attn_low = jnp.dot(grad_branch, w_out.T, preferred_element_type=jnp.float32).astype(
        jnp.bfloat16
    )
    other = [bits[1], bits[0]] + bits[2:]
    last = bits[2:3] + bits[:2] + bits[3:]
    flow_down = RowScatter(grad_w_down, last)
    flow_gate = RowScatter(grad_w_gate, bits)
    flow_up = RowScatter(grad_w_up, other)
    flow_out = RowScatter(grad_w_out, other)
    flows = [flow_down, flow_gate, flow_up, flow_out]
    for flow in flows:
        flow.stage()
    grad_query_low, grad_key_values = attend_back(attended, log_total, grad_attn_low)
    cur = grad_key_values.reshape(seq_count, seq_len, 2 * head_dim)
    for bit in bits:
        half = cur.shape[1] // 2
        total = cur[:, :half].astype(jnp.float32) + swap(cur[:, half:], "ctx", bit).astype(
            jnp.float32
        )
        cur = total if bit == bits[-1] else total.astype(jnp.bfloat16)
    grad_keys_own = cur[:, :, :head_dim]
    grad_values_own = cur[:, :, head_dim:]
    flow_query = RowScatter(
        jnp.dot(normed.T, grad_query_low, preferred_element_type=jnp.float32), bits
    )
    flow_query.stage()
    grad_key_low = (
        rotate(grad_keys_own.reshape(seq_count, half_rows, 1, head_dim), cos_table, -sin_table)
        .reshape(tok_rows, head_dim)
        .astype(jnp.bfloat16)
    )
    grad_value_low = grad_values_own.reshape(tok_rows, head_dim).astype(jnp.bfloat16)
    grad_w_key = jnp.dot(normed.T, grad_key_low, preferred_element_type=jnp.float32)
    grad_w_value = jnp.dot(normed.T, grad_value_low, preferred_element_type=jnp.float32)
    grad_b_query = jnp.sum(grad_query_low.astype(jnp.float32), axis=0)
    grad_b_key = jnp.sum(grad_key_low.astype(jnp.float32), axis=0)
    grad_b_value = jnp.sum(grad_value_low.astype(jnp.float32), axis=0)
    grad_first_part = (
        jnp.dot(grad_query_low, w_query.T, preferred_element_type=jnp.float32)
        + jnp.dot(grad_key_low, w_key.T, preferred_element_type=jnp.float32)
        + jnp.dot(grad_value_low, w_value.T, preferred_element_type=jnp.float32)
    )
    flows = flows + [flow_query]
    grad_w_pair = jnp.concatenate([grad_w_key, grad_w_value], axis=1).astype(jnp.bfloat16)
    first_low, grad_w_pair = in_step(
        flows, grad_first_part.astype(jnp.bfloat16), grad_w_pair
    )
    for flow in flows:
        flow.stage()
    flow_pair = RowScatter(grad_w_pair, other)
    flow_pair.stage()
    flow_pair.stage()
    grad_normed = sum_pair(first_low)
    grad_in_part, grad_attn_gain = norm_back(grad_normed, x_float, inv_one, gain_one)
    grad_tokens = grad_stream + grad_in_part
    sum_down = flow_down.finish().T
    sum_gate = flow_gate.finish()
    sum_up = flow_up.finish()
    sum_out = flow_out.finish().T
    sum_query = flow_query.finish()
    key_value_sum = flow_pair.finish()
    sum_key = key_value_sum[:, :head_dim]
    sum_value = key_value_sum[:, head_dim:]
    pieces = (grad_attn_gain, grad_mlp_gain, grad_b_query, grad_b_key, grad_b_value)
    flat = jnp.concatenate(pieces)
    padded = -(-flat.shape[0] // 1024) * 1024
    flat = jnp.pad(flat, (0, padded - flat.shape[0])).reshape(8, padded // 8)
    for bit in bits:
        flat = flat + swap(flat, "ctx", bit)
    flat = flat.reshape(padded)
    small = []
    begin = 0
    for piece in pieces:
        small.append(flat[begin : begin + piece.shape[0]])
        begin += piece.shape[0]
    return (
        mixed,
        grad_tokens,
        small[0],
        sum_query,
        small[2],
        sum_key,
        small[3],
        sum_value,
        small[4],
        sum_out,
        small[1],
        sum_gate,
        sum_up,
        sum_down,
    )


def solution(mesh):
    return jax.shard_map(
        shards,
        mesh=mesh,
        in_specs=(
            P("ctx", None),
            P(),
            P(None, "tp"),
            P("tp"),
            P(None, "tp"),
            P("tp"),
            P(None, "tp"),
            P("tp"),
            P("tp", None),
            P(),
            P(None, "tp"),
            P(None, "tp"),
            P("tp", None),
            P("ctx", None),
            P(),
            P(),
        ),
        out_specs=(
            P("ctx", None),
            P("ctx", None),
            P(),
            P("ctx", "tp"),
            P("tp"),
            P("ctx", "tp"),
            P("tp"),
            P("ctx", "tp"),
            P("tp"),
            P("tp", "ctx"),
            P(),
            P("ctx", "tp"),
            P("ctx", "tp"),
            P("tp", "ctx"),
        ),
        check_vma=False,
    )
```
